32 devices in a mesh: seq: 16 (over z, y, x), tp: 2 (over core).
Axes of the slice: x: 2, y: 2, z: 4, core: 2. Of those that a mesh axis runs over, the one named last changes fastest.
Arguments:
- segment_ids: int32 [4096], replicated, may hold values from 0 to 7, never falling along the last dimension, each value on 1 to 1024 neighbouring positions
- relayout: int32 [4096], replicated, may hold values from 0 to 4095, as said below
- queries: bfloat16 [4096, 4096], P('seq', 'tp'), may hold values from -8 to 8
- keys: bfloat16 [4096, 512], P(('seq', 'tp')), may hold values from -8 to 8
- values: bfloat16 [4096, 512], P(('seq', 'tp')), may hold values from -18 to 18
- out_weight: bfloat16 [4096, 8192], P('tp'), may hold values from -0.09375 to 0.09375
Outputs:
- block_out: bfloat16 [4096, 8192], P(('seq', 'tp'))
The draws below stay inside these ranges and needn't reach their ends.
Inputs may be any that keep to these rules, and one draw needn't show every extreme that they name: relayout is a permutation; of the 256 tokens in each aligned block of 256 initial positions exactly 16 land in each aligned block of 256 new positions.
All inputs are finite; a program needn't handle non-finite values.
Results may differ from the reference program's by a relative error of at most 0.017.
Values may be sent and summed in bfloat16 or wider, within the bound.
A program may use at most 192 MiB of HBM per device.

```python
import math
import jax
import jax.numpy as jnp
import numpy as np
from jax import lax

D = 8192
QH = 32
KVH = 4
HD = 128
TOK_DEV = 256
TOKENS = 4096
MOST_LEN = 1024
DOCS = 8
N_TP = 2


def query_key_pair(key):
    base = jax.random.fold_in(key, 11)
    key_query, key_key = jax.random.split(base, 2)
    query_draw = jax.random.normal(key_query, (TOKENS, QH * HD), jnp.float32)
    key_draw = jax.random.normal(key_key, (TOKENS, KVH * HD), jnp.float32)
    return (jnp.clip(query_draw, -8.0, 8.0), jnp.clip(key_draw, -8.0, 8.0))


def draw_queries(key, part):
    return query_key_pair(key)[0].astype(jnp.bfloat16)


def draw_keys(key, part):
    return query_key_pair(key)[1].astype(jnp.bfloat16)


def draw_relayout(key, part):
    base = jax.random.fold_in(key, 23)
    key_first, key_second = jax.random.split(base, 2)
    positions = jnp.arange(TOKENS, dtype=jnp.int32)
    blocks = TOKENS // TOK_DEV
    source = positions // TOK_DEV
    shuffle_first = jax.random.permutation(key_first, TOKENS).astype(jnp.int32)
    order = jnp.argsort(source * TOKENS + shuffle_first)
    ranks = jnp.zeros((TOKENS,), jnp.int32).at[order].set(positions % TOK_DEV)
    target = ranks % blocks
    shuffle_second = jax.random.permutation(key_second, TOKENS).astype(jnp.int32)
    return jnp.argsort(target * TOKENS + shuffle_second).astype(jnp.int32)


def level_of(rng, extent, shards, smallest, high):
    factor_of, own = 1.0, jax.random.fold_in(rng, 6)
    for position, parts in shards:
        heights = jnp.exp(jax.random.uniform(jax.random.fold_in(own, position), (parts,), jnp.float32, smallest / len(shards), high / len(shards)))
        factor_of = factor_of * jnp.repeat(heights, extent[position] // parts).reshape([-1 if axis == position else 1 for axis in range(len(extent))])
    return factor_of


def split_up(count, total, most, lean):
    loads = [(1 << 20) // math.isqrt(grade ** lean) + 1 for grade in range(2, count + 1)]
    rest, given = total - most - (count - 1), [1] * (count - 1)
    while rest > 0:
        candidates = [i for i in range(count - 1) if given[i] < most]
        mass, budget = sum([loads[i] for i in candidates]), rest
        for i in candidates:
            addition = min(most - given[i], max(1, budget * loads[i] // mass), rest)
            given[i] = given[i] + addition
            rest = rest - addition
    return np.array([most] + given)


def uneven_parts(own_key, amount, total, most, lean):
    if amount == 2:
        one = jax.random.randint(own_key, (), max(1, total - most), min(most, total - 1) + 1)
        return jnp.stack([one, total - one])
    sizes = jnp.asarray(split_up(amount, total, most, lean), jnp.int32)
    twos = (amount - 1) // 2
    source_of, sink = sizes[1:1 + 2 * twos:2], sizes[2:2 + 2 * twos:2]
    margin = jnp.minimum(source_of - 1, most - sink)
    moved = jax.random.randint(jax.random.fold_in(own_key, 1), (twos,), 0, 1 << 20) % (margin + 1)
    sizes = sizes.at[1:1 + 2 * twos:2].set(source_of - moved).at[2:2 + 2 * twos:2].set(sink + moved)
    return sizes[jax.random.permutation(jax.random.fold_in(own_key, 2), amount)]


def noise(own_key, dims, scale, most, cuts=(), kind=jnp.bfloat16):
    array = jax.random.normal(own_key, dims, jnp.float32) * scale
    if len(cuts) > 0:
        array = level_of(own_key, dims, cuts, -0.22, 0.18) * array
    return jnp.clip(array, min=-most, max=most).astype(kind)


def setup_inputs(seed: int = 0) -> dict:
    splits = jax.random.split(jax.random.key(seed), 7)
    segment_ids = jnp.searchsorted(jnp.cumsum(uneven_parts(splits[0], DOCS, TOKENS, MOST_LEN, 1)), jnp.arange(TOKENS), side="right").astype(jnp.int32)
    relayout = draw_relayout(jax.random.fold_in(splits[6], 71), 0)
    queries = draw_queries(jax.random.fold_in(splits[6], 71), 0)
    keys = draw_keys(jax.random.fold_in(splits[6], 71), 0)
    values = noise(splits[4], (TOKENS, KVH * HD), 3.0, 18.0, ((0, 32),))
    out_weight = noise(splits[5], (QH * HD, D), (QH * HD) ** -0.5, 0.09375, ((0, 2),))
    return {"segment_ids": segment_ids, "relayout": relayout, "queries": queries, "keys": keys, "values": values, "out_weight": out_weight}


def reference(segment_ids, relayout, queries, keys, values, out_weight):
    group = QH // KVH
    block = math.gcd(TOKENS, 512)
    reach = MOST_LEN
    scale = HD ** -0.5
    query_heads = queries.reshape(TOKENS, KVH, group, HD)
    key_pad = jnp.concatenate([jnp.zeros((reach, KVH * HD), jnp.bfloat16), keys], axis=0).reshape(TOKENS + reach, KVH, HD)
    value_pad = jnp.concatenate([jnp.zeros((reach, KVH * HD), jnp.bfloat16), values], axis=0).reshape(TOKENS + reach, KVH, HD)
    seg_pad = jnp.concatenate([jnp.full((reach,), -1, jnp.int32), segment_ids], axis=0)

    def one_block(index):
        start = (index * block).astype(jnp.int32)
        q_block = lax.dynamic_slice_in_dim(query_heads, start, block, 0).astype(jnp.float32)
        k_block = lax.dynamic_slice_in_dim(key_pad, start, reach + block, 0).astype(jnp.float32)
        v_block = lax.dynamic_slice_in_dim(value_pad, start, reach + block, 0).astype(jnp.float32)
        q_pos = start + jnp.arange(block, dtype=jnp.int32)
        q_seg = lax.dynamic_slice_in_dim(segment_ids, start, block, 0)
        k_pos = start - reach + jnp.arange(reach + block, dtype=jnp.int32)
        k_seg = lax.dynamic_slice_in_dim(seg_pad, start, reach + block, 0)
        live = (k_pos[None, :] <= q_pos[:, None]) & (k_seg[None, :] == q_seg[:, None]) & (k_pos[None, :] >= 0)
        scores = jnp.einsum("qngd,knd->ngqk", q_block, k_block) * scale
        masked = jnp.where(live, scores, jnp.float32(-1e30))
        peak = jnp.max(masked, axis=-1, keepdims=True)
        expo = jnp.where(live, jnp.exp(masked - peak), jnp.float32(0.0))
        denom = jnp.sum(expo, axis=-1)
        weight = lax.optimization_barrier(expo.astype(jnp.bfloat16)).astype(jnp.float32)
        summed = jnp.einsum("ngqk,knd->ngqd", weight, v_block)
        attn = summed / denom[..., None]
        return jnp.transpose(attn, (2, 0, 1, 3)).reshape(block, QH * HD).astype(jnp.bfloat16)

    attn_all = lax.map(one_block, jnp.arange(TOKENS // block, dtype=jnp.int32)).reshape(TOKENS, QH * HD)
    relaid = attn_all[relayout]
    width = QH * HD // N_TP
    result = jnp.zeros((TOKENS, D), jnp.float32)
    for group_index in range(N_TP):
        part = jnp.dot(relaid[:, group_index * width:(group_index + 1) * width], out_weight[group_index * width:(group_index + 1) * width], preferred_element_type=jnp.float32)
        result = result + part.astype(jnp.bfloat16).astype(jnp.float32)
    return result.astype(jnp.bfloat16)
```

```python
import functools

import jax
import jax.numpy as jnp
from jax import lax
from jax.experimental import pallas as pl
from jax.experimental.pallas import tpu as pltpu
from jax.sharding import PartitionSpec as P

QH = 32
KVH = 4
HD = 128
LONGEST_SHARE = 4
MESH = pl.DeviceIdType.MESH
WIDE = 512
PIECES = 8


def dot(a, b):
    return jnp.dot(a, b, preferred_element_type=jnp.float32)


def dot_nt(a, b):
    return lax.dot_general(a, b, (((1,), (1,)), ((), ())), preferred_element_type=jnp.float32)


def loop(low, high, body):
    def step(i, carry):
        body(i)
        return carry

    lax.fori_loop(low, high, step, 0)


def fused_kernel(
    n, reach, seg_ref, lay_ref, q_ref, k_ref, v_ref, w_hbm, out_ref,
    kv, stage, bias, send_perm, recv_perm, rank_ref, mixed, sendb, arr, acc, part, other, wbuf,
    w_sem, pair_send, pair_recv, far_send, far_recv, near_send, near_recv,
    a2a_send, a2a_recv, sum_send, sum_recv,
):
    s = lax.axis_index("seq")
    t = lax.axis_index("tp")
    rows = q_ref.shape[0]
    half = rows // 2
    per_pair = rows // n
    shared = kv.shape[1]
    per_shared = q_ref.shape[1] // HD // shared
    depth = per_shared * HD
    wide_count = acc.shape[0]
    w_rows = w_hbm.shape[0] // PIECES
    place = lax.rem(s, reach)
    base = s - place

    def w_copy(i):
        cut = pl.ds(pl.multiple_of(i * w_rows, w_rows), w_rows)
        return pltpu.make_async_copy(w_hbm.at[cut], wbuf.at[cut], w_sem.at[i])

    loop(0, PIECES, lambda i: w_copy(i).start())

    own_half = pl.ds(pl.multiple_of(t * half, half), half)
    other_half = pl.ds(pl.multiple_of((1 - t) * half, half), half)
    for g in range(shared):
        mine = pl.ds(pl.multiple_of((t * shared + g) * HD, HD), HD)
        theirs = pl.ds(pl.multiple_of(((1 - t) * shared + g) * HD, HD), HD)
        kv[0, g, own_half, 0:HD] = k_ref[:, mine]
        kv[0, g, own_half, HD : 2 * HD] = v_ref[:, mine]
        stage[g, :, 0:HD] = k_ref[:, theirs]
        stage[g, :, HD : 2 * HD] = v_ref[:, theirs]

    barrier = pltpu.get_barrier_semaphore()
    loop(
        1, n,
        lambda e: pl.semaphore_signal(
            barrier, inc=1, device_id={"seq": lax.rem(s + e, n)}, device_id_type=MESH
        ),
    )
    pl.semaphore_signal(barrier, inc=1, device_id={"tp": 1 - t}, device_id_type=MESH)
    pl.semaphore_wait(barrier, n)

    def pair_copy(g):
        return pltpu.make_async_remote_copy(
            src_ref=stage.at[g], dst_ref=kv.at[0, g, own_half],
            send_sem=pair_send.at[g], recv_sem=pair_recv.at[g],
            device_id={"tp": 1 - t}, device_id_type=MESH,
        )

    def far_copy(g):
        return pltpu.make_async_remote_copy(
            src_ref=kv.at[0, g], dst_ref=kv.at[reach, g],
            send_sem=far_send.at[g], recv_sem=far_recv.at[g],
            device_id={"seq": lax.rem(s + reach, n)}, device_id_type=MESH,
        )

    def near_copy(g, e, slot):
        return pltpu.make_async_remote_copy(
            src_ref=kv.at[slot, g], dst_ref=kv.at[e, g],
            send_sem=near_send.at[g, e], recv_sem=near_recv.at[g, e],
            device_id={"seq": base + lax.rem(place + e, reach)}, device_id_type=MESH,
        )

    def own_out(g):
        pair_copy(g).wait_recv()

        @pl.when(s + reach < n)
        def _():
            far_copy(g).start()

        for e in range(1, reach):

            @pl.when(place + e < reach)
            def _():
                near_copy(g, e, 0).start()

    def relay(g):
        @pl.when(s >= reach)
        def _():
            far_copy(g).wait_recv()
            for e in range(1, reach):

                @pl.when(place + e >= reach)
                def _():
                    near_copy(g, e, reach).start()

    for g in range(shared):
        pair_copy(g).start()
    for e in range(1, reach + 1):

        @pl.when(s < e)
        def _():
            kv[e] = jnp.zeros_like(kv[e])

    own_out(0)

    row_id = lax.broadcasted_iota(jnp.int32, (rows, rows), 0)
    col_id = lax.broadcasted_iota(jnp.int32, (rows, rows), 1)
    query_seg = jnp.broadcast_to(seg_ref[pl.ds(s, 1), :], (rows, rows)).T
    for d in range(reach + 1):
        key_seg = seg_ref[pl.ds(jnp.maximum(s - d, 0), 1), :]
        live = query_seg == jnp.where(s >= d, key_seg, -1)
        if d == 0:
            live = live & (col_id <= row_id)
        bias[d] = jnp.where(live, jnp.float32(0.0), jnp.float32(-1e30))

    relay(0)
    for g in range(1, shared):
        own_out(g)

    before = jnp.where(row_id < col_id, 1.0, 0.0).astype(jnp.bfloat16)
    local = lay_ref[...] - s * rows
    is_mine = (local >= 0) & (local < rows)
    ranks = dot(jnp.where(is_mine, 1.0, 0.0).astype(jnp.bfloat16), before)
    rank_ref[...] = jnp.where(is_mine, ranks, -1.0)
    rank_id = lax.broadcasted_iota(jnp.int32, (per_pair, rows), 0).astype(jnp.float32)

    def one_target(b):
        pick = jnp.where(rank_ref[pl.ds(b, 1), :] == rank_id, 1.0, 0.0).astype(jnp.bfloat16)
        token = jnp.where(lay_ref[pl.ds(b, 1), :] - s * rows == row_id, 1.0, 0.0).astype(jnp.bfloat16)
        cut = pl.ds(pl.multiple_of(b * per_pair, per_pair), per_pair)
        send_perm[cut, :] = dot_nt(pick, token).astype(jnp.bfloat16)

    loop(0, n, one_target)
    origin = lay_ref[pl.ds(s, 1), :] // rows
    block_id = lax.broadcasted_iota(jnp.int32, (n, rows), 0)
    from_block = jnp.where(origin == block_id, 1.0, 0.0)
    earlier = dot(from_block.astype(jnp.bfloat16), before)
    rank = jnp.sum(from_block * earlier, axis=0, keepdims=True)
    slot_of = origin.astype(jnp.float32) * per_pair + rank
    slot_col = jnp.broadcast_to(slot_of, (rows, rows)).T
    recv_perm[...] = jnp.where(slot_col == col_id.astype(jnp.float32), 1.0, 0.0).astype(jnp.bfloat16)

    for g in range(1, shared):
        relay(g)

    def a2a_copy(g, e):
        target = lax.rem(s + e, n)
        return pltpu.make_async_remote_copy(
            src_ref=sendb.at[g, pl.ds(pl.multiple_of(target * per_pair, per_pair), per_pair)],
            dst_ref=arr.at[g, pl.ds(pl.multiple_of(s * per_pair, per_pair), per_pair)],
            send_sem=a2a_send.at[g, e], recv_sem=a2a_recv.at[g, e],
            device_id={"seq": target}, device_id_type=MESH,
        )

    factor = HD ** (-0.5) * 1.4426950408889634

    for g in range(shared):
        for e in range(1, reach):

            @pl.when(s >= e)
            def _():
                near_copy(g, e, 0).wait_recv()

        def one_head(h):
            q = q_ref[:, pl.ds(pl.multiple_of((g * per_shared + h) * HD, HD), HD)]
            scores = [dot_nt(q, kv[d, g, :, 0:HD]) + bias[d] for d in range(reach + 1)]
            peak = jnp.max(functools.reduce(jnp.maximum, scores), axis=1, keepdims=True)
            expo = [jnp.exp2((x - peak) * factor) for x in scores]
            denom = jnp.sum(functools.reduce(jnp.add, expo), axis=1, keepdims=True)
            update = functools.reduce(
                jnp.add,
                [dot(x.astype(jnp.bfloat16), kv[d, g, :, HD : 2 * HD]) for d, x in enumerate(expo)],
            )
            attn = (update / denom).astype(jnp.bfloat16)
            sendb[g, :, pl.ds(pl.multiple_of(h * HD, HD), HD)] = dot(
                send_perm[...], attn
            ).astype(jnp.bfloat16)

        loop(0, per_shared, one_head)
        loop(1, n, lambda e: a2a_copy(g, e).start())
        keep = pl.ds(pl.multiple_of(s * per_pair, per_pair), per_pair)
        arr[g, keep, :] = sendb[g, keep, :]

    def sum_copy(c):
        return pltpu.make_async_remote_copy(
            src_ref=part.at[c, other_half], dst_ref=other.at[c],
            send_sem=sum_send.at[c], recv_sem=sum_recv.at[c],
            device_id={"tp": 1 - t}, device_id_type=MESH,
        )

    for g in range(shared):
        share = PIECES // shared
        loop(g * share, (g + 1) * share, lambda i: w_copy(i).wait())
        loop(1, n, lambda e: a2a_copy(g, e).wait_recv())
        mixed[...] = dot(recv_perm[...], arr[g]).astype(jnp.bfloat16)

        def one_width(c):
            cut = pl.ds(pl.multiple_of(c * WIDE, WIDE), WIDE)
            term = dot(mixed[...], wbuf[g * depth : (g + 1) * depth, cut])
            if g > 0:
                term = term + acc[c]
            if g < shared - 1:
                acc[c] = term
            else:
                part[c] = term.astype(jnp.bfloat16)
                sum_copy(c).start()

        loop(0, wide_count, one_width)

    def finish(c):
        sum_copy(c).wait_recv()
        total = part[c, own_half, :].astype(jnp.float32) + other[c].astype(jnp.float32)
        out_ref[:, pl.ds(pl.multiple_of(c * WIDE, WIDE), WIDE)] = total.astype(jnp.bfloat16)

    loop(0, wide_count, finish)

    for g in range(shared):
        pair_copy(g).wait_send()

        @pl.when(s + reach < n)
        def _():
            far_copy(g).wait_send()

        for e in range(1, reach):

            @pl.when((place + e < reach) | (s >= reach))
            def _():
                near_copy(g, e, 0).wait_send()

        loop(1, n, lambda e: a2a_copy(g, e).wait_send())
    loop(0, wide_count, lambda c: sum_copy(c).wait_send())


def fused_shards(segment_ids, relayout, queries, keys, values, out_weight):
    n = lax.axis_size("seq")
    rows = queries.shape[0]
    reach = n // LONGEST_SHARE
    shared = keys.shape[1] // HD // 2
    depth = queries.shape[1] // shared
    width = out_weight.shape[1]
    wide_count = width // WIDE
    bf16, f32 = jnp.bfloat16, jnp.float32
    dma = pltpu.SemaphoreType.DMA
    vmem = pl.BlockSpec(memory_space=pltpu.VMEM)
    return pl.pallas_call(
        functools.partial(fused_kernel, n, reach),
        out_shape=jax.ShapeDtypeStruct((rows // 2, width), bf16),
        in_specs=[vmem] * 5 + [pl.BlockSpec(memory_space=pl.ANY)],
        out_specs=vmem,
        scratch_shapes=[
            pltpu.VMEM((reach + 1, shared, rows, 2 * HD), bf16),
            pltpu.VMEM((shared, rows // 2, 2 * HD), bf16),
            pltpu.VMEM((reach + 1, rows, rows), f32),
            pltpu.VMEM((rows, rows), bf16),
            pltpu.VMEM((rows, rows), bf16),
            pltpu.VMEM((n, rows), f32),
            pltpu.VMEM((rows, depth), bf16),
            pltpu.VMEM((shared, rows, depth), bf16),
            pltpu.VMEM((shared, rows, depth), bf16),
            pltpu.VMEM((wide_count, rows, WIDE), f32),
            pltpu.VMEM((wide_count, rows, WIDE), bf16),
            pltpu.VMEM((wide_count, rows // 2, WIDE), bf16),
            pltpu.VMEM(out_weight.shape, bf16),
            dma((PIECES,)),
            dma((shared,)),
            dma((shared,)),
            dma((shared,)),
            dma((shared,)),
            dma((shared, reach)),
            dma((shared, reach)),
            dma((shared, n)),
            dma((shared, n)),
            dma((wide_count,)),
            dma((wide_count,)),
        ],
        compiler_params=pltpu.CompilerParams(
            collective_id=0, has_side_effects=True, vmem_limit_bytes=63 * 1024 * 1024
        ),
    )(segment_ids.reshape(n, rows), relayout.reshape(n, rows), queries, keys, values, out_weight)


def shards(segment_ids, relayout, queries, keys, values, out_weight):
    rows_here = queries.shape[0]
    seq_count = lax.axis_size("seq")
    seq_index = lax.axis_index("seq")
    tp_index = lax.axis_index("tp")
    total_rows = rows_here * seq_count
    heads_here = queries.shape[1] // HD
    group = QH // KVH
    shared_here = max(1, heads_here // group)
    per_shared = heads_here // shared_here
    scale = HD ** (-0.5)
    all_keys, all_values = (
        lax.all_gather(keys, "tp", axis=0, tiled=True),
        lax.all_gather(values, "tp", axis=0, tiled=True),
    )
    first_head = tp_index * heads_here // group
    own_keys = lax.dynamic_slice_in_dim(all_keys, first_head * HD, shared_here * HD, 1)
    own_values = lax.dynamic_slice_in_dim(all_values, first_head * HD, shared_here * HD, 1)
    own_pair = jnp.stack([own_keys, own_values])
    row_ids = jnp.arange(rows_here, dtype=jnp.int32)
    inverse = (
        jnp.zeros((total_rows,), jnp.int32)
        .at[relayout]
        .set(jnp.arange(total_rows, dtype=jnp.int32))
    )
    new_here = seq_index * rows_here + row_ids
    old_here = seq_index * rows_here + row_ids
    source_block = relayout[new_here] // rows_here
    arrival = jnp.argsort(source_block * total_rows + new_here)
    send_order = jnp.argsort(inverse[old_here])
    arrived = lax.all_to_all(queries[send_order], "seq", split_axis=0, concat_axis=0, tiled=True)
    query_pos = relayout[seq_index * rows_here + arrival]
    query_seg = segment_ids[query_pos]
    pieces = lax.all_gather(own_pair, "seq", axis=1, tiled=True)
    count = pieces.shape[1]
    key_pos = jnp.arange(count, dtype=jnp.int32)
    live = (
        (key_pos[None, :] <= query_pos[:, None])
        & (segment_ids[None, :] == query_seg[:, None])
        & (jnp.int32(0) >= 0)
    )
    query_split = arrived.reshape(rows_here, shared_here, per_shared, HD)
    key_split = pieces[0].reshape(count, shared_here, HD)
    value_split = pieces[1].reshape(count, shared_here, HD)
    scores = (
        jnp.einsum("qngd,knd->ngqk", query_split, key_split, preferred_element_type=jnp.float32)
        * scale
    )
    masked = jnp.where(live, scores, jnp.float32(-1e30))
    peak = jnp.full((shared_here, per_shared, rows_here), -1e30, jnp.float32)
    new_peak = jnp.maximum(peak, jnp.max(masked, axis=-1))
    expo = jnp.where(live, jnp.exp(masked - new_peak[..., None]), jnp.float32(0.0))
    denom = jnp.sum(expo, axis=-1)
    update = jnp.einsum(
        "ngqk,knd->ngqd", expo.astype(jnp.bfloat16), value_split, preferred_element_type=jnp.float32
    )
    attn = update / denom[..., None]
    attn_rows = (
        jnp.transpose(attn, (2, 0, 1, 3)).reshape(rows_here, heads_here * HD).astype(jnp.bfloat16)
    )
    attn_new = jnp.zeros_like(attn_rows).at[arrival].set(attn_rows)
    return lax.psum_scatter(
        jnp.dot(attn_new, out_weight, preferred_element_type=jnp.float32).astype(jnp.bfloat16),
        "tp",
        scatter_dimension=0,
        tiled=True,
    )


def solution(mesh):
    return jax.shard_map(
        fused_shards if mesh.shape["tp"] == 2 else shards,
        mesh=mesh,
        in_specs=(
            P(),
            P(),
            P("seq", "tp"),
            P(("seq", "tp"), None),
            P(("seq", "tp"), None),
            P("tp", None),
        ),
        out_specs=P(("seq", "tp"), None),
        check_vma=False,
    )
```

```python
import functools

import jax
import jax.numpy as jnp
from jax import lax
from jax.experimental import pallas as pl
from jax.experimental.pallas import tpu as pltpu
from jax.sharding import PartitionSpec as P

QH = 32
KVH = 4
HD = 128
LONGEST_SHARE = 4
MESH = pl.DeviceIdType.MESH
WIDE = 512
PIECES = 8
CUTS = 4
TOGETHER = 2


def dot(a, b):
    return jnp.dot(a, b, preferred_element_type=jnp.float32)


def dot_nt(a, b):
    return lax.dot_general(a, b, (((1,), (1,)), ((), ())), preferred_element_type=jnp.float32)


def loop(low, high, body):
    def step(i, carry):
        body(i)
        return carry

    lax.fori_loop(low, high, step, 0)


def fused_kernel(
    n, reach, seg_in, lay_in, q_ref, k_ref, v_ref, w_hbm, own_out_ref, other_ref,
    seg_ref, lay_ref, kv, stage, key_tag, query_tag, own_first, send_perm, recv_perm, rank_ref, q_sorted,
    mixed, sendb, arr, acc, part, wbuf,
    w_sem, pair_send, pair_recv, far_send, far_recv, near_send, near_recv,
    a2a_send, a2a_recv, sum_send, sum_recv, keep_sem,
):
    s = lax.axis_index("seq")
    t = lax.axis_index("tp")
    rows = q_ref.shape[0]
    half = rows // 2
    per_pair = rows // n
    shared = kv.shape[1]
    per_shared = q_ref.shape[1] // HD // shared
    cuts, _, depth = sendb.shape
    cut_heads = depth // HD
    wide_count = acc.shape[0]
    w_rows = w_hbm.shape[0] // PIECES
    place = lax.rem(s, reach)
    base = s - place

    barrier = pltpu.get_barrier_semaphore()
    loop(
        1, n,
        lambda e: pl.semaphore_signal(
            barrier, inc=1, device_id={"seq": lax.rem(s + e, n)}, device_id_type=MESH
        ),
    )
    pl.semaphore_signal(barrier, inc=1, device_id={"tp": 1 - t}, device_id_type=MESH)

    def w_copy(i):
        cut = pl.ds(pl.multiple_of(i * w_rows, w_rows), w_rows)
        return pltpu.make_async_copy(w_hbm.at[cut], wbuf.at[cut], w_sem.at[i])

    loop(0, PIECES, lambda i: w_copy(i).start())

    own_half = pl.ds(pl.multiple_of(t * half, half), half)
    other_half = pl.ds(pl.multiple_of((1 - t) * half, half), half)
    for g in range(shared):
        mine = pl.ds(pl.multiple_of((t * shared + g) * HD, HD), HD)
        theirs = pl.ds(pl.multiple_of(((1 - t) * shared + g) * HD, HD), HD)
        kv[0, g, own_half, 0:HD] = k_ref[:, mine]
        kv[0, g, own_half, HD : 2 * HD] = v_ref[:, mine]
        stage[g, :, 0:HD] = k_ref[:, theirs]
        stage[g, :, HD : 2 * HD] = v_ref[:, theirs]

    pl.semaphore_wait(barrier, n)

    def pair_copy(g):
        return pltpu.make_async_remote_copy(
            src_ref=stage.at[g], dst_ref=kv.at[0, g, own_half],
            send_sem=pair_send.at[g], recv_sem=pair_recv.at[g],
            device_id={"tp": 1 - t}, device_id_type=MESH,
        )

    def far_copy(g):
        return pltpu.make_async_remote_copy(
            src_ref=kv.at[0, g], dst_ref=kv.at[reach, g],
            send_sem=far_send.at[g], recv_sem=far_recv.at[g],
            device_id={"seq": lax.rem(s + reach, n)}, device_id_type=MESH,
        )

    def near_copy(g, e, slot):
        return pltpu.make_async_remote_copy(
            src_ref=kv.at[slot, g], dst_ref=kv.at[e, g],
            send_sem=near_send.at[g, e], recv_sem=near_recv.at[g, e],
            device_id={"seq": base + lax.rem(place + e, reach)}, device_id_type=MESH,
        )

    def own_out(g):
        pair_copy(g).wait_recv()

        @pl.when(s + reach < n)
        def _():
            far_copy(g).start()

        for e in range(1, reach):

            @pl.when(place + e < reach)
            def _():
                near_copy(g, e, 0).start()

    def relay(g):
        @pl.when(s >= reach)
        def _():
            far_copy(g).wait_recv()
            for e in range(1, reach):

                @pl.when(place + e >= reach)
                def _():
                    near_copy(g, e, reach).start()

    for g in range(shared):
        pair_copy(g).start()
    for e in range(1, reach + 1):

        @pl.when(s < e)
        def _():
            kv[e] = jnp.zeros_like(kv[e])

    own_out(0)

    lines = rows // 128
    for ref, source in ((seg_ref, seg_in), (lay_ref, lay_in)):
        for i in range(lines):
            ref[:, i * 128 : (i + 1) * 128] = source[pl.ds(i, n, stride=lines), :]

    tag_id = lax.broadcasted_iota(jnp.int32, (rows, HD), 1)
    for d in range(reach + 1):
        key_seg = jnp.where(s >= d, seg_ref[pl.ds(jnp.maximum(s - d, 0), 1), :], HD - 1)
        key_col = jnp.broadcast_to(key_seg, (HD, rows)).T
        key_tag[d] = jnp.where(key_col == tag_id, 1.0, 0.0).astype(jnp.bfloat16)

    relay(0)
    for g in range(1, shared):
        own_out(g)

    row_id = lax.broadcasted_iota(jnp.int32, (rows, rows), 0)
    col_id = lax.broadcasted_iota(jnp.int32, (rows, rows), 1)

    before = jnp.where(row_id < col_id, 1.0, 0.0).astype(jnp.bfloat16)
    local = lay_ref[...] - s * rows
    is_mine = (local >= 0) & (local < rows)
    ranks = dot(jnp.where(is_mine, 1.0, 0.0).astype(jnp.bfloat16), before)
    rank_ref[...] = jnp.where(is_mine, ranks, -1.0)
    rank_id = lax.broadcasted_iota(jnp.int32, (per_pair, rows), 0).astype(jnp.float32)

    def one_target(b):
        pick = jnp.where(rank_ref[pl.ds(b, 1), :] == rank_id, 1.0, 0.0).astype(jnp.bfloat16)
        token = jnp.where(lay_ref[pl.ds(b, 1), :] - s * rows == row_id, 1.0, 0.0).astype(jnp.bfloat16)
        cut = pl.ds(pl.multiple_of(b * per_pair, per_pair), per_pair)
        send_perm[cut, :] = dot_nt(pick, token).astype(jnp.bfloat16)

    loop(0, n, one_target)

    def sort_queries(c):
        cut = pl.ds(pl.multiple_of(c * depth, depth), depth)
        q_sorted[:, cut] = dot(send_perm[...], q_ref[:, cut]).astype(jnp.bfloat16)

    loop(0, cuts, sort_queries)
    chosen = send_perm[...].astype(jnp.float32)
    position = jnp.sum(chosen * col_id.astype(jnp.float32), axis=1, keepdims=True)
    document = jnp.sum(chosen * seg_ref[pl.ds(s, 1), :].astype(jnp.float32), axis=1, keepdims=True)
    query_tag[...] = jnp.where(document == tag_id.astype(jnp.float32), 0.0, -1e30).astype(jnp.bfloat16)
    own_first[...] = jnp.where(col_id.astype(jnp.float32) <= position, 1.0, 0.0)

    origin = lay_ref[pl.ds(s, 1), :] // rows
    block_id = lax.broadcasted_iota(jnp.int32, (n, rows), 0)
    from_block = jnp.where(origin == block_id, 1.0, 0.0)
    earlier = dot(from_block.astype(jnp.bfloat16), before)
    rank = jnp.sum(from_block * earlier, axis=0, keepdims=True)
    slot_of = origin.astype(jnp.float32) * per_pair + rank
    slot_col = jnp.broadcast_to(slot_of, (rows, rows)).T
    recv_perm[...] = jnp.where(slot_col == col_id.astype(jnp.float32), 1.0, 0.0).astype(jnp.bfloat16)

    for g in range(1, shared):
        relay(g)

    def a2a_copy(g, e):
        target = lax.rem(s + e, n)
        return pltpu.make_async_remote_copy(
            src_ref=sendb.at[g, pl.ds(pl.multiple_of(target * per_pair, per_pair), per_pair)],
            dst_ref=arr.at[g, pl.ds(pl.multiple_of(s * per_pair, per_pair), per_pair)],
            send_sem=a2a_send.at[g, e], recv_sem=a2a_recv.at[g, e],
            device_id={"seq": target}, device_id_type=MESH,
        )

    factor = HD ** (-0.5) * 1.4426950408889634

    ones = jnp.ones((rows, HD), jnp.bfloat16)

    def one_head(g, h, to):
        q = q_sorted[:, pl.ds(pl.multiple_of(h * HD, HD), HD)]
        q = jnp.concatenate([q, query_tag[...]], axis=1)
        scores = [
            dot_nt(q, jnp.concatenate([kv[d, g, :, 0:HD], key_tag[d]], axis=1)) for d in range(reach + 1)
        ]
        is_own = own_first[...] > 0.5
        scores = [jnp.where(is_own, scores[0], scores[reach])] + scores[1:reach]
        peak = jnp.max(functools.reduce(jnp.maximum, scores), axis=1, keepdims=True)
        expo = [jnp.exp2((x - peak) * factor) for x in scores]
        expo = (
            [jnp.where(is_own, expo[0], 0.0)] + expo[1:] + [jnp.where(is_own, 0.0, expo[0])]
        )
        update = functools.reduce(
            jnp.add,
            [
                dot(x.astype(jnp.bfloat16), jnp.concatenate([kv[d, g, :, HD : 2 * HD], ones], axis=1))
                for d, x in enumerate(expo)
            ],
        )
        sendb[to, :, pl.ds(pl.multiple_of((h - to * cut_heads) * HD, HD), HD)] = (
            update[:, 0:HD] / update[:, HD : 2 * HD]
        ).astype(jnp.bfloat16)

    for c in range(cuts):
        g = c * cut_heads // per_shared
        if c * cut_heads % per_shared == 0:
            for e in range(1, reach):

                @pl.when(s >= e)
                def _():
                    near_copy(g, e, 0).wait_recv()

        def heads(i):
            for k in range(TOGETHER):
                one_head(g, c * cut_heads + i * TOGETHER + k, c)

        loop(0, cut_heads // TOGETHER, heads)
        loop(1, n, lambda e: a2a_copy(c, e).start())
        keep = pl.ds(pl.multiple_of(s * per_pair, per_pair), per_pair)
        arr[c, keep, :] = sendb[c, keep, :]

    def wide_cut(c):
        return pl.ds(pl.multiple_of(c * WIDE, WIDE), WIDE)

    def sum_copy(c):
        return pltpu.make_async_remote_copy(
            src_ref=part.at[c, other_half], dst_ref=other_ref.at[:, wide_cut(c)],
            send_sem=sum_send.at[c], recv_sem=sum_recv.at[c],
            device_id={"tp": 1 - t}, device_id_type=MESH,
        )

    def keep_copy(c):
        return pltpu.make_async_copy(part.at[c, own_half], own_out_ref.at[:, wide_cut(c)], keep_sem.at[c])

    for g in range(cuts):
        share = PIECES // cuts
        loop(g * share, (g + 1) * share, lambda i: w_copy(i).wait())
        loop(1, n, lambda e: a2a_copy(g, e).wait_recv())
        mixed[...] = dot(recv_perm[...], arr[g]).astype(jnp.bfloat16)

        def one_width(c):
            term = dot(mixed[...], wbuf[g * depth : (g + 1) * depth, wide_cut(c)])
            if g > 0:
                term = term + acc[c]
            if g < cuts - 1:
                acc[c] = term
            else:
                part[c] = term.astype(jnp.bfloat16)
                sum_copy(c).start()
                keep_copy(c).start()

        loop(0, wide_count, one_width)

    def finish(c):
        keep_copy(c).wait()
        sum_copy(c).wait_recv()

    loop(0, wide_count, finish)

    for g in range(shared):
        pair_copy(g).wait_send()

        @pl.when(s + reach < n)
        def _():
            far_copy(g).wait_send()

        for e in range(1, reach):

            @pl.when((place + e < reach) | (s >= reach))
            def _():
                near_copy(g, e, 0).wait_send()

    for c in range(cuts):
        loop(1, n, lambda e: a2a_copy(c, e).wait_send())
    loop(0, wide_count, lambda c: sum_copy(c).wait_send())


def fused_shards(segment_ids, relayout, queries, keys, values, out_weight):
    n = lax.axis_size("seq")
    rows = queries.shape[0]
    reach = n // LONGEST_SHARE
    shared = keys.shape[1] // HD // 2
    depth = queries.shape[1] // CUTS
    width = out_weight.shape[1]
    wide_count = width // WIDE
    bf16, f32 = jnp.bfloat16, jnp.float32
    dma = pltpu.SemaphoreType.DMA
    vmem = pl.BlockSpec(memory_space=pltpu.VMEM)
    own, other = pl.pallas_call(
        functools.partial(fused_kernel, n, reach),
        out_shape=[jax.ShapeDtypeStruct((rows // 2, width), bf16)] * 2,
        in_specs=[vmem] * 5 + [pl.BlockSpec(memory_space=pl.ANY)],
        out_specs=[pl.BlockSpec(memory_space=pl.ANY)] * 2,
        scratch_shapes=[
            pltpu.VMEM((n, rows), jnp.int32),
            pltpu.VMEM((n, rows), jnp.int32),
            pltpu.VMEM((reach + 1, shared, rows, 2 * HD), bf16),
            pltpu.VMEM((shared, rows // 2, 2 * HD), bf16),
            pltpu.VMEM((reach + 1, rows, HD), bf16),
            pltpu.VMEM((rows, HD), bf16),
            pltpu.VMEM((rows, rows), f32),
            pltpu.VMEM((rows, rows), bf16),
            pltpu.VMEM((rows, rows), bf16),
            pltpu.VMEM((n, rows), f32),
            pltpu.VMEM(queries.shape, bf16),
            pltpu.VMEM((rows, depth), bf16),
            pltpu.VMEM((CUTS, rows, depth), bf16),
            pltpu.VMEM((CUTS, rows, depth), bf16),
            pltpu.VMEM((wide_count, rows, WIDE), f32),
            pltpu.VMEM((wide_count, rows, WIDE), bf16),
            pltpu.VMEM(out_weight.shape, bf16),
            dma((PIECES,)),
            dma((shared,)),
            dma((shared,)),
            dma((shared,)),
            dma((shared,)),
            dma((shared, reach)),
            dma((shared, reach)),
            dma((CUTS, n)),
            dma((CUTS, n)),
            dma((wide_count,)),
            dma((wide_count,)),
            dma((wide_count,)),
        ],
        compiler_params=pltpu.CompilerParams(
            collective_id=0, has_side_effects=True, vmem_limit_bytes=63 * 1024 * 1024
        ),
    )(segment_ids.reshape(-1, 128), relayout.reshape(-1, 128), queries, keys, values, out_weight)
    return (own.astype(f32) + other.astype(f32)).astype(bf16)


def shards(segment_ids, relayout, queries, keys, values, out_weight):
    rows_here = queries.shape[0]
    seq_count = lax.axis_size("seq")
    seq_index = lax.axis_index("seq")
    tp_index = lax.axis_index("tp")
    total_rows = rows_here * seq_count
    heads_here = queries.shape[1] // HD
    group = QH // KVH
    shared_here = max(1, heads_here // group)
    per_shared = heads_here // shared_here
    scale = HD ** (-0.5)
    all_keys, all_values = (
        lax.all_gather(keys, "tp", axis=0, tiled=True),
        lax.all_gather(values, "tp", axis=0, tiled=True),
    )
    first_head = tp_index * heads_here // group
    own_keys = lax.dynamic_slice_in_dim(all_keys, first_head * HD, shared_here * HD, 1)
    own_values = lax.dynamic_slice_in_dim(all_values, first_head * HD, shared_here * HD, 1)
    own_pair = jnp.stack([own_keys, own_values])
    row_ids = jnp.arange(rows_here, dtype=jnp.int32)
    inverse = (
        jnp.zeros((total_rows,), jnp.int32)
        .at[relayout]
        .set(jnp.arange(total_rows, dtype=jnp.int32))
    )
    new_here = seq_index * rows_here + row_ids
    old_here = seq_index * rows_here + row_ids
    source_block = relayout[new_here] // rows_here
    arrival = jnp.argsort(source_block * total_rows + new_here)
    send_order = jnp.argsort(inverse[old_here])
    arrived = lax.all_to_all(queries[send_order], "seq", split_axis=0, concat_axis=0, tiled=True)
    query_pos = relayout[seq_index * rows_here + arrival]
    query_seg = segment_ids[query_pos]
    pieces = lax.all_gather(own_pair, "seq", axis=1, tiled=True)
    count = pieces.shape[1]
    key_pos = jnp.arange(count, dtype=jnp.int32)
    live = (
        (key_pos[None, :] <= query_pos[:, None])
        & (segment_ids[None, :] == query_seg[:, None])
        & (jnp.int32(0) >= 0)
    )
    query_split = arrived.reshape(rows_here, shared_here, per_shared, HD)
    key_split = pieces[0].reshape(count, shared_here, HD)
    value_split = pieces[1].reshape(count, shared_here, HD)
    scores = (
        jnp.einsum("qngd,knd->ngqk", query_split, key_split, preferred_element_type=jnp.float32)
        * scale
    )
    masked = jnp.where(live, scores, jnp.float32(-1e30))
    peak = jnp.full((shared_here, per_shared, rows_here), -1e30, jnp.float32)
    new_peak = jnp.maximum(peak, jnp.max(masked, axis=-1))
    expo = jnp.where(live, jnp.exp(masked - new_peak[..., None]), jnp.float32(0.0))
    denom = jnp.sum(expo, axis=-1)
    update = jnp.einsum(
        "ngqk,knd->ngqd", expo.astype(jnp.bfloat16), value_split, preferred_element_type=jnp.float32
    )
    attn = update / denom[..., None]
    attn_rows = (
        jnp.transpose(attn, (2, 0, 1, 3)).reshape(rows_here, heads_here * HD).astype(jnp.bfloat16)
    )
    attn_new = jnp.zeros_like(attn_rows).at[arrival].set(attn_rows)
    return lax.psum_scatter(
        jnp.dot(attn_new, out_weight, preferred_element_type=jnp.float32).astype(jnp.bfloat16),
        "tp",
        scatter_dimension=0,
        tiled=True,
    )


def solution(mesh):
    return jax.shard_map(
        fused_shards if mesh.shape["tp"] == 2 else shards,
        mesh=mesh,
        in_specs=(
            P(),
            P(),
            P("seq", "tp"),
            P(("seq", "tp"), None),
            P(("seq", "tp"), None),
            P("tp", None),
        ),
        out_specs=P(("seq", "tp"), None),
        check_vma=False,
    )
```

```python
import functools

import jax
import jax.numpy as jnp
from jax import lax
from jax.experimental import pallas as pl
from jax.experimental.pallas import tpu as pltpu
from jax.sharding import PartitionSpec as P

QH = 32
KVH = 4
HD = 128
LONGEST_SHARE = 4
MESH = pl.DeviceIdType.MESH
WIDE = 512
PIECES = 32
CUTS = 4
TOGETHER = 2
BEHIND = 3
COPIES = 8


def dot(a, b):
    return jnp.dot(a, b, preferred_element_type=jnp.float32)


def dot_nt(a, b):
    return lax.dot_general(a, b, (((1,), (1,)), ((), ())), preferred_element_type=jnp.float32)


def loop(low, high, body):
    def step(i, carry):
        body(i)
        return carry

    lax.fori_loop(low, high, step, 0)


def fused_kernel(
    n, reach, seg_in, lay_in, q_ref, k_ref, v_ref, w_hbm, out_ref,
    seg_ref, lay_ref, kv, stage, key_tag, query_tag, own_first, send_perm, recv_perm, rank_ref, q_sorted,
    mixed, sendb, arr, acc, part, other, wbuf,
    w_sem, pair_send, pair_recv, far_send, far_recv, near_send, near_recv,
    a2a_send, a2a_recv, sum_send, sum_recv, keep_sem,
):
    s = lax.axis_index("seq")
    t = lax.axis_index("tp")
    rows = q_ref.shape[0]
    half = rows // 2
    per_pair = rows // n
    shared = kv.shape[1]
    per_shared = q_ref.shape[1] // HD // shared
    cuts, _, depth = sendb.shape
    cut_heads = depth // HD
    wide_count = acc.shape[0]
    w_rows = w_hbm.shape[0] // PIECES
    place = lax.rem(s, reach)
    base = s - place

    barrier = pltpu.get_barrier_semaphore()
    loop(
        1, n,
        lambda e: pl.semaphore_signal(
            barrier, inc=1, device_id={"seq": lax.rem(s + e, n)}, device_id_type=MESH
        ),
    )
    pl.semaphore_signal(barrier, inc=1, device_id={"tp": 1 - t}, device_id_type=MESH)

    def w_copy(i):
        cut = pl.ds(pl.multiple_of(i * w_rows, w_rows), w_rows)
        return pltpu.make_async_copy(w_hbm.at[cut], wbuf.at[cut], w_sem.at[i])

    own_half = pl.ds(pl.multiple_of(t * half, half), half)
    other_half = pl.ds(pl.multiple_of((1 - t) * half, half), half)
    for g in range(shared):
        mine = pl.ds(pl.multiple_of((t * shared + g) * HD, HD), HD)
        theirs = pl.ds(pl.multiple_of(((1 - t) * shared + g) * HD, HD), HD)
        kv[0, g, own_half, 0:HD] = k_ref[:, mine]
        kv[0, g, own_half, HD : 2 * HD] = v_ref[:, mine]
        stage[g, :, 0:HD] = k_ref[:, theirs]
        stage[g, :, HD : 2 * HD] = v_ref[:, theirs]

    pl.semaphore_wait(barrier, n)

    def pair_copy(g):
        return pltpu.make_async_remote_copy(
            src_ref=stage.at[g], dst_ref=kv.at[0, g, own_half],
            send_sem=pair_send.at[g], recv_sem=pair_recv.at[g],
            device_id={"tp": 1 - t}, device_id_type=MESH,
        )

    def far_copy(g):
        return pltpu.make_async_remote_copy(
            src_ref=kv.at[0, g], dst_ref=kv.at[reach, g],
            send_sem=far_send.at[g], recv_sem=far_recv.at[g],
            device_id={"seq": lax.rem(s + reach, n)}, device_id_type=MESH,
        )

    def near_copy(g, e, slot):
        return pltpu.make_async_remote_copy(
            src_ref=kv.at[slot, g], dst_ref=kv.at[e, g],
            send_sem=near_send.at[g, e], recv_sem=near_recv.at[g, e],
            device_id={"seq": base + lax.rem(place + e, reach)}, device_id_type=MESH,
        )

    def own_out(g):
        pair_copy(g).wait_recv()

        @pl.when(s + reach < n)
        def _():
            far_copy(g).start()

        for e in range(1, reach):

            @pl.when(place + e < reach)
            def _():
                near_copy(g, e, 0).start()

    def relay(g):
        @pl.when(s >= reach)
        def _():
            far_copy(g).wait_recv()
            for e in range(1, reach):

                @pl.when(place + e >= reach)
                def _():
                    near_copy(g, e, reach).start()

    for g in range(shared):
        pair_copy(g).start()
    for e in range(1, reach + 1):

        @pl.when(s < e)
        def _():
            kv[e] = jnp.zeros_like(kv[e])

    own_out(0)

    lines = rows // 128
    for ref, source in ((seg_ref, seg_in), (lay_ref, lay_in)):
        for i in range(lines):
            ref[:, i * 128 : (i + 1) * 128] = source[pl.ds(i, n, stride=lines), :]

    tag_id = lax.broadcasted_iota(jnp.int32, (rows, HD), 1)
    for d in range(reach + 1):
        key_seg = jnp.where(s >= d, seg_ref[pl.ds(jnp.maximum(s - d, 0), 1), :], HD - 1)
        key_col = jnp.broadcast_to(key_seg, (HD, rows)).T
        key_tag[d] = jnp.where(key_col == tag_id, 1.0, 0.0).astype(jnp.bfloat16)

    relay(0)
    for g in range(1, shared):
        own_out(g)

    row_id = lax.broadcasted_iota(jnp.int32, (rows, rows), 0)
    col_id = lax.broadcasted_iota(jnp.int32, (rows, rows), 1)

    before = jnp.where(row_id < col_id, 1.0, 0.0).astype(jnp.bfloat16)
    local = lay_ref[...] - s * rows
    is_mine = (local >= 0) & (local < rows)
    ranks = dot(jnp.where(is_mine, 1.0, 0.0).astype(jnp.bfloat16), before)
    rank_ref[...] = jnp.where(is_mine, ranks, -1.0)
    rank_id = lax.broadcasted_iota(jnp.int32, (per_pair, rows), 0).astype(jnp.float32)

    def one_target(b):
        pick = jnp.where(rank_ref[pl.ds(b, 1), :] == rank_id, 1.0, 0.0).astype(jnp.bfloat16)
        token = jnp.where(lay_ref[pl.ds(b, 1), :] - s * rows == row_id, 1.0, 0.0).astype(jnp.bfloat16)
        cut = pl.ds(pl.multiple_of(b * per_pair, per_pair), per_pair)
        send_perm[cut, :] = dot_nt(pick, token).astype(jnp.bfloat16)

    loop(0, n, one_target)

    def sort_queries(c):
        cut = pl.ds(pl.multiple_of(c * depth, depth), depth)
        q_sorted[:, cut] = dot(send_perm[...], q_ref[:, cut]).astype(jnp.bfloat16)

    loop(0, cuts, sort_queries)
    chosen = send_perm[...].astype(jnp.float32)
    position = jnp.sum(chosen * col_id.astype(jnp.float32), axis=1, keepdims=True)
    document = jnp.sum(chosen * seg_ref[pl.ds(s, 1), :].astype(jnp.float32), axis=1, keepdims=True)
    query_tag[...] = jnp.where(document == tag_id.astype(jnp.float32), 0.0, -1e30).astype(jnp.bfloat16)
    own_first[...] = jnp.where(col_id.astype(jnp.float32) <= position, 1.0, 0.0)

    origin = lay_ref[pl.ds(s, 1), :] // rows
    block_id = lax.broadcasted_iota(jnp.int32, (n, rows), 0)
    from_block = jnp.where(origin == block_id, 1.0, 0.0)
    earlier = dot(from_block.astype(jnp.bfloat16), before)
    rank = jnp.sum(from_block * earlier, axis=0, keepdims=True)
    slot_of = origin.astype(jnp.float32) * per_pair + rank
    slot_col = jnp.broadcast_to(slot_of, (rows, rows)).T
    recv_perm[...] = jnp.where(slot_col == col_id.astype(jnp.float32), 1.0, 0.0).astype(jnp.bfloat16)

    for g in range(1, shared):
        relay(g)

    def a2a_copy(g, e):
        target = lax.rem(s + e, n)
        return pltpu.make_async_remote_copy(
            src_ref=sendb.at[g, pl.ds(pl.multiple_of(target * per_pair, per_pair), per_pair)],
            dst_ref=arr.at[g, pl.ds(pl.multiple_of(s * per_pair, per_pair), per_pair)],
            send_sem=a2a_send.at[g, e], recv_sem=a2a_recv.at[g, e],
            device_id={"seq": target}, device_id_type=MESH,
        )

    factor = HD ** (-0.5) * 1.4426950408889634

    ones = jnp.ones((rows, HD), jnp.bfloat16)

    def one_head(g, h, to):
        q = q_sorted[:, pl.ds(pl.multiple_of(h * HD, HD), HD)]
        q = jnp.concatenate([q, query_tag[...]], axis=1)
        scores = [
            dot_nt(q, jnp.concatenate([kv[d, g, :, 0:HD], key_tag[d]], axis=1)) for d in range(reach + 1)
        ]
        is_own = own_first[...] > 0.5
        scores = [jnp.where(is_own, scores[0], scores[reach])] + scores[1:reach]
        peak = jnp.max(functools.reduce(jnp.maximum, scores), axis=1, keepdims=True)
        expo = [jnp.exp2((x - peak) * factor) for x in scores]
        expo = (
            [jnp.where(is_own, expo[0], 0.0)] + expo[1:] + [jnp.where(is_own, 0.0, expo[0])]
        )
        update = functools.reduce(
            jnp.add,
            [
                dot(x.astype(jnp.bfloat16), jnp.concatenate([kv[d, g, :, HD : 2 * HD], ones], axis=1))
                for d, x in enumerate(expo)
            ],
        )
        sendb[to, :, pl.ds(pl.multiple_of((h - to * cut_heads) * HD, HD), HD)] = (
            update[:, 0:HD] / update[:, HD : 2 * HD]
        ).astype(jnp.bfloat16)

    for c in range(cuts):
        g = c * cut_heads // per_shared
        if c * cut_heads % per_shared == 0:
            for e in range(1, reach):

                @pl.when(s >= e)
                def _():
                    near_copy(g, e, 0).wait_recv()

        def heads(i):
            w_step = PIECES * TOGETHER // (cuts * cut_heads)
            first = (c * cut_heads // TOGETHER + i) * w_step
            loop(first, first + w_step, lambda j: w_copy(j).start())
            for k in range(TOGETHER):
                one_head(g, c * cut_heads + i * TOGETHER + k, c)

        loop(0, cut_heads // TOGETHER, heads)
        loop(1, n, lambda e: a2a_copy(c, e).start())
        keep = pl.ds(pl.multiple_of(s * per_pair, per_pair), per_pair)
        arr[c, keep, :] = sendb[c, keep, :]

    def wide_cut(c):
        return pl.ds(pl.multiple_of(c * WIDE, WIDE), WIDE)

    def sum_copy(c):
        return pltpu.make_async_remote_copy(
            src_ref=part.at[c, other_half], dst_ref=other.at[c],
            send_sem=sum_send.at[c], recv_sem=sum_recv.at[c],
            device_id={"tp": 1 - t}, device_id_type=MESH,
        )

    def keep_copy(c):
        return pltpu.make_async_copy(part.at[c, own_half], out_ref.at[:, wide_cut(c)], keep_sem.at[c])

    def finish(c):
        sum_copy(c).wait_recv()
        total = part[c, own_half, :].astype(jnp.float32) + other[c].astype(jnp.float32)
        part[c, own_half, :] = total.astype(jnp.bfloat16)
        keep_copy(c).start()

    for g in range(cuts):
        share = PIECES // cuts
        loop(g * share, (g + 1) * share, lambda i: w_copy(i).wait())
        loop(1, n, lambda e: a2a_copy(g, e).wait_recv())
        mixed[...] = dot(recv_perm[...], arr[g]).astype(jnp.bfloat16)

        def one_width(c):
            term = dot(mixed[...], wbuf[g * depth : (g + 1) * depth, wide_cut(c)])
            if g > 0:
                term = term + acc[c]
            if g < cuts - 1:
                acc[c] = term
            else:
                part[c] = term.astype(jnp.bfloat16)
                sum_copy(c).start()

                @pl.when(c >= BEHIND)
                def _():
                    finish(c - BEHIND)

        loop(0, wide_count, one_width)

    loop(wide_count - BEHIND, wide_count, finish)
    loop(0, wide_count, lambda c: keep_copy(c).wait())

    for g in range(shared):
        pair_copy(g).wait_send()

        @pl.when(s + reach < n)
        def _():
            far_copy(g).wait_send()

        for e in range(1, reach):

            @pl.when((place + e < reach) | (s >= reach))
            def _():
                near_copy(g, e, 0).wait_send()

    for c in range(cuts):
        loop(1, n, lambda e: a2a_copy(c, e).wait_send())
    loop(0, wide_count, lambda c: sum_copy(c).wait_send())


def copy_kernel(from_ref, to_ref, sem):
    rows = from_ref.shape[0] // COPIES
    copies = [
        pltpu.make_async_copy(from_ref.at[pl.ds(i * rows, rows)], to_ref.at[pl.ds(i * rows, rows)], sem.at[i])
        for i in range(COPIES)
    ]
    for copy in copies:
        copy.start()
    for copy in copies:
        copy.wait()


def fused_shards(segment_ids, relayout, queries, keys, values, out_weight):
    n = lax.axis_size("seq")
    rows = queries.shape[0]
    reach = n // LONGEST_SHARE
    shared = keys.shape[1] // HD // 2
    depth = queries.shape[1] // CUTS
    width = out_weight.shape[1]
    wide_count = width // WIDE
    bf16, f32 = jnp.bfloat16, jnp.float32
    dma = pltpu.SemaphoreType.DMA
    vmem = pl.BlockSpec(memory_space=pltpu.VMEM)
    result = pl.pallas_call(
        functools.partial(fused_kernel, n, reach),
        out_shape=jax.ShapeDtypeStruct((rows // 2, width), bf16),
        in_specs=[vmem] * 5 + [pl.BlockSpec(memory_space=pl.ANY)],
        out_specs=pl.BlockSpec(memory_space=pl.ANY),
        scratch_shapes=[
            pltpu.VMEM((n, rows), jnp.int32),
            pltpu.VMEM((n, rows), jnp.int32),
            pltpu.VMEM((reach + 1, shared, rows, 2 * HD), bf16),
            pltpu.VMEM((shared, rows // 2, 2 * HD), bf16),
            pltpu.VMEM((reach + 1, rows, HD), bf16),
            pltpu.VMEM((rows, HD), bf16),
            pltpu.VMEM((rows, rows), f32),
            pltpu.VMEM((rows, rows), bf16),
            pltpu.VMEM((rows, rows), bf16),
            pltpu.VMEM((n, rows), f32),
            pltpu.VMEM(queries.shape, bf16),
            pltpu.VMEM((rows, depth), bf16),
            pltpu.VMEM((CUTS, rows, depth), bf16),
            pltpu.VMEM((CUTS, rows, depth), bf16),
            pltpu.VMEM((wide_count, rows, WIDE), f32),
            pltpu.VMEM((wide_count, rows, WIDE), bf16),
            pltpu.VMEM((wide_count, rows // 2, WIDE), bf16),
            pltpu.VMEM(out_weight.shape, bf16),
            dma((PIECES,)),
            dma((shared,)),
            dma((shared,)),
            dma((shared,)),
            dma((shared,)),
            dma((shared, reach)),
            dma((shared, reach)),
            dma((CUTS, n)),
            dma((CUTS, n)),
            dma((wide_count,)),
            dma((wide_count,)),
            dma((wide_count,)),
        ],
        compiler_params=pltpu.CompilerParams(
            collective_id=0, has_side_effects=True, vmem_limit_bytes=63 * 1024 * 1024
        ),
    )(segment_ids.reshape(-1, 128), relayout.reshape(-1, 128), queries, keys, values, out_weight)
    return pl.pallas_call(
        copy_kernel,
        out_shape=jax.ShapeDtypeStruct(result.shape, bf16),
        in_specs=[pl.BlockSpec(memory_space=pl.ANY)],
        out_specs=pl.BlockSpec(memory_space=pl.ANY),
        scratch_shapes=[dma((COPIES,))],
    )(result)


def shards(segment_ids, relayout, queries, keys, values, out_weight):
    rows_here = queries.shape[0]
    seq_count = lax.axis_size("seq")
    seq_index = lax.axis_index("seq")
    tp_index = lax.axis_index("tp")
    total_rows = rows_here * seq_count
    heads_here = queries.shape[1] // HD
    group = QH // KVH
    shared_here = max(1, heads_here // group)
    per_shared = heads_here // shared_here
    scale = HD ** (-0.5)
    all_keys, all_values = (
        lax.all_gather(keys, "tp", axis=0, tiled=True),
        lax.all_gather(values, "tp", axis=0, tiled=True),
    )
    first_head = tp_index * heads_here // group
    own_keys = lax.dynamic_slice_in_dim(all_keys, first_head * HD, shared_here * HD, 1)
    own_values = lax.dynamic_slice_in_dim(all_values, first_head * HD, shared_here * HD, 1)
    own_pair = jnp.stack([own_keys, own_values])
    row_ids = jnp.arange(rows_here, dtype=jnp.int32)
    inverse = (
        jnp.zeros((total_rows,), jnp.int32)
        .at[relayout]
        .set(jnp.arange(total_rows, dtype=jnp.int32))
    )
    new_here = seq_index * rows_here + row_ids
    old_here = seq_index * rows_here + row_ids
    source_block = relayout[new_here] // rows_here
    arrival = jnp.argsort(source_block * total_rows + new_here)
    send_order = jnp.argsort(inverse[old_here])
    arrived = lax.all_to_all(queries[send_order], "seq", split_axis=0, concat_axis=0, tiled=True)
    query_pos = relayout[seq_index * rows_here + arrival]
    query_seg = segment_ids[query_pos]
    pieces = lax.all_gather(own_pair, "seq", axis=1, tiled=True)
    count = pieces.shape[1]
    key_pos = jnp.arange(count, dtype=jnp.int32)
    live = (
        (key_pos[None, :] <= query_pos[:, None])
        & (segment_ids[None, :] == query_seg[:, None])
        & (jnp.int32(0) >= 0)
    )
    query_split = arrived.reshape(rows_here, shared_here, per_shared, HD)
    key_split = pieces[0].reshape(count, shared_here, HD)
    value_split = pieces[1].reshape(count, shared_here, HD)
    scores = (
        jnp.einsum("qngd,knd->ngqk", query_split, key_split, preferred_element_type=jnp.float32)
        * scale
    )
    masked = jnp.where(live, scores, jnp.float32(-1e30))
    peak = jnp.full((shared_here, per_shared, rows_here), -1e30, jnp.float32)
    new_peak = jnp.maximum(peak, jnp.max(masked, axis=-1))
    expo = jnp.where(live, jnp.exp(masked - new_peak[..., None]), jnp.float32(0.0))
    denom = jnp.sum(expo, axis=-1)
    update = jnp.einsum(
        "ngqk,knd->ngqd", expo.astype(jnp.bfloat16), value_split, preferred_element_type=jnp.float32
    )
    attn = update / denom[..., None]
    attn_rows = (
        jnp.transpose(attn, (2, 0, 1, 3)).reshape(rows_here, heads_here * HD).astype(jnp.bfloat16)
    )
    attn_new = jnp.zeros_like(attn_rows).at[arrival].set(attn_rows)
    return lax.psum_scatter(
        jnp.dot(attn_new, out_weight, preferred_element_type=jnp.float32).astype(jnp.bfloat16),
        "tp",
        scatter_dimension=0,
        tiled=True,
    )


def solution(mesh):
    return jax.shard_map(
        fused_shards if mesh.shape["tp"] == 2 else shards,
        mesh=mesh,
        in_specs=(
            P(),
            P(),
            P("seq", "tp"),
            P(("seq", "tp"), None),
            P(("seq", "tp"), None),
            P("tp", None),
        ),
        out_specs=P(("seq", "tp"), None),
        check_vma=False,
    )
```

```python
import functools

import jax
import jax.numpy as jnp
from jax import lax
from jax.experimental import pallas as pl
from jax.experimental.pallas import tpu as pltpu
from jax.sharding import PartitionSpec as P

QH = 32
KVH = 4
HD = 128
LONGEST_SHARE = 4
MESH = pl.DeviceIdType.MESH
WIDE = 512
PIECES = 32
CUTS = 4
TOGETHER = 2
BEHIND = 3
COPIES = 8


def dot(a, b):
    return jnp.dot(a, b, preferred_element_type=jnp.float32)


def dot_nt(a, b):
    return lax.dot_general(a, b, (((1,), (1,)), ((), ())), preferred_element_type=jnp.float32)


def loop(low, high, body):
    def step(i, carry):
        body(i)
        return carry

    lax.fori_loop(low, high, step, 0)


def fused_kernel(
    n, reach, seg_in, lay_in, q_ref, k_ref, v_ref, w_hbm, out_ref,
    seg_ref, lay_ref, kv, stage, key_tag, query_tag, own_first, send_perm, recv_perm, rank_ref, q_sorted,
    mixed, sendb, arr, acc, part, other, wbuf,
    w_sem, pair_send, pair_recv, far_send, far_recv, near_send, near_recv,
    a2a_send, a2a_recv, sum_send, sum_recv, keep_sem,
):
    s = lax.axis_index("seq")
    t = lax.axis_index("tp")
    rows = q_ref.shape[0]
    half = rows // 2
    per_pair = rows // n
    shared = kv.shape[1]
    per_shared = q_ref.shape[1] // HD // shared
    cuts, _, depth = sendb.shape
    cut_heads = depth // HD
    wide_count = acc.shape[0]
    w_rows = w_hbm.shape[0] // PIECES
    place = lax.rem(s, reach)
    base = s - place

    barrier = pltpu.get_barrier_semaphore()
    loop(
        1, n,
        lambda e: pl.semaphore_signal(
            barrier, inc=1, device_id={"seq": lax.rem(s + e, n)}, device_id_type=MESH
        ),
    )
    pl.semaphore_signal(barrier, inc=1, device_id={"tp": 1 - t}, device_id_type=MESH)

    def w_copy(i):
        cut = pl.ds(pl.multiple_of(i * w_rows, w_rows), w_rows)
        return pltpu.make_async_copy(w_hbm.at[cut], wbuf.at[cut], w_sem.at[i])

    own_half = pl.ds(pl.multiple_of(t * half, half), half)
    other_half = pl.ds(pl.multiple_of((1 - t) * half, half), half)
    for g in range(shared):
        mine = pl.ds(pl.multiple_of((t * shared + g) * HD, HD), HD)
        theirs = pl.ds(pl.multiple_of(((1 - t) * shared + g) * HD, HD), HD)
        kv[0, g, own_half, 0:HD] = k_ref[:, mine]
        kv[0, g, own_half, HD : 2 * HD] = v_ref[:, mine]
        stage[g, :, 0:HD] = k_ref[:, theirs]
        stage[g, :, HD : 2 * HD] = v_ref[:, theirs]

    pl.semaphore_wait(barrier, n)

    def pair_copy(g):
        return pltpu.make_async_remote_copy(
            src_ref=stage.at[g], dst_ref=kv.at[0, g, own_half],
            send_sem=pair_send.at[g], recv_sem=pair_recv.at[g],
            device_id={"tp": 1 - t}, device_id_type=MESH,
        )

    def far_copy(g):
        return pltpu.make_async_remote_copy(
            src_ref=kv.at[0, g], dst_ref=kv.at[reach, g],
            send_sem=far_send.at[g], recv_sem=far_recv.at[g],
            device_id={"seq": lax.rem(s + reach, n)}, device_id_type=MESH,
        )

    def near_copy(g, e, slot):
        return pltpu.make_async_remote_copy(
            src_ref=kv.at[slot, g], dst_ref=kv.at[e, g],
            send_sem=near_send.at[g, e], recv_sem=near_recv.at[g, e],
            device_id={"seq": base + lax.rem(place + e, reach)}, device_id_type=MESH,
        )

    def own_out(g):
        pair_copy(g).wait_recv()

        @pl.when(s + reach < n)
        def _():
            far_copy(g).start()

        for e in range(1, reach):

            @pl.when(place + e < reach)
            def _():
                near_copy(g, e, 0).start()

    def relay(g):
        @pl.when(s >= reach)
        def _():
            far_copy(g).wait_recv()
            for e in range(1, reach):

                @pl.when(place + e >= reach)
                def _():
                    near_copy(g, e, reach).start()

    for g in range(shared):
        pair_copy(g).start()
    for e in range(1, reach + 1):

        @pl.when(s < e)
        def _():
            kv[e] = jnp.zeros_like(kv[e])

    own_out(0)

    lines = rows // 128
    for ref, source in ((seg_ref, seg_in), (lay_ref, lay_in)):
        for i in range(lines):
            ref[:, i * 128 : (i + 1) * 128] = source[pl.ds(i, n, stride=lines), :]

    tag_id = lax.broadcasted_iota(jnp.int32, (rows, HD), 1)
    for d in range(reach + 1):
        key_seg = jnp.where(s >= d, seg_ref[pl.ds(jnp.maximum(s - d, 0), 1), :], HD - 1)
        key_col = jnp.broadcast_to(key_seg, (HD, rows)).T
        key_tag[d] = jnp.where(key_col == tag_id, 1.0, 0.0).astype(jnp.bfloat16)

    relay(0)
    for g in range(1, shared):
        own_out(g)

    row_id = lax.broadcasted_iota(jnp.int32, (rows, rows), 0)
    col_id = lax.broadcasted_iota(jnp.int32, (rows, rows), 1)

    before = jnp.where(row_id < col_id, 1.0, 0.0).astype(jnp.bfloat16)
    local = lay_ref[...] - s * rows
    is_mine = (local >= 0) & (local < rows)
    ranks = dot(jnp.where(is_mine, 1.0, 0.0).astype(jnp.bfloat16), before)
    rank_ref[...] = jnp.where(is_mine, ranks, -1.0)
    rank_id = lax.broadcasted_iota(jnp.int32, (per_pair, rows), 0).astype(jnp.float32)

    def one_target(b):
        pick = jnp.where(rank_ref[pl.ds(b, 1), :] == rank_id, 1.0, 0.0).astype(jnp.bfloat16)
        token = jnp.where(lay_ref[pl.ds(b, 1), :] - s * rows == row_id, 1.0, 0.0).astype(jnp.bfloat16)
        cut = pl.ds(pl.multiple_of(b * per_pair, per_pair), per_pair)
        send_perm[cut, :] = dot_nt(pick, token).astype(jnp.bfloat16)

    loop(0, n, one_target)

    def sort_queries(c):
        cut = pl.ds(pl.multiple_of(c * depth, depth), depth)
        q_sorted[:, cut] = dot(send_perm[...], q_ref[:, cut]).astype(jnp.bfloat16)

    loop(0, cuts, sort_queries)
    chosen = send_perm[...].astype(jnp.float32)
    position = jnp.sum(chosen * col_id.astype(jnp.float32), axis=1, keepdims=True)
    document = jnp.sum(chosen * seg_ref[pl.ds(s, 1), :].astype(jnp.float32), axis=1, keepdims=True)
    query_tag[...] = jnp.where(document == tag_id.astype(jnp.float32), 0.0, -1e30).astype(jnp.bfloat16)
    own_first[...] = jnp.where(col_id.astype(jnp.float32) <= position, 1.0, 0.0)

    origin = lay_ref[pl.ds(s, 1), :] // rows
    block_id = lax.broadcasted_iota(jnp.int32, (n, rows), 0)
    from_block = jnp.where(origin == block_id, 1.0, 0.0)
    earlier = dot(from_block.astype(jnp.bfloat16), before)
    rank = jnp.sum(from_block * earlier, axis=0, keepdims=True)
    slot_of = origin.astype(jnp.float32) * per_pair + rank
    slot_col = jnp.broadcast_to(slot_of, (rows, rows)).T
    recv_perm[...] = jnp.where(slot_col == col_id.astype(jnp.float32), 1.0, 0.0).astype(jnp.bfloat16)

    for g in range(1, shared):
        relay(g)

    def a2a_copy(g, e):
        target = lax.rem(s + e, n)
        return pltpu.make_async_remote_copy(
            src_ref=sendb.at[g, pl.ds(pl.multiple_of(target * per_pair, per_pair), per_pair)],
            dst_ref=arr.at[g, pl.ds(pl.multiple_of(s * per_pair, per_pair), per_pair)],
            send_sem=a2a_send.at[g, e], recv_sem=a2a_recv.at[g, e],
            device_id={"seq": target}, device_id_type=MESH,
        )

    factor = HD ** (-0.5) * 1.4426950408889634

    ones = jnp.ones((rows, HD), jnp.bfloat16)

    def some_heads(g, h, to):
        q = [q_sorted[:, pl.ds(pl.multiple_of((h + k) * HD, HD), HD)] for k in range(TOGETHER)]
        q = jnp.concatenate([jnp.concatenate([x, query_tag[...]], axis=1) for x in q], axis=0)
        scores = [
            dot_nt(q, jnp.concatenate([kv[d, g, :, 0:HD], key_tag[d]], axis=1)) for d in range(reach + 1)
        ]
        is_own = jnp.concatenate([own_first[...]] * TOGETHER, axis=0) > 0.5
        scores = [jnp.where(is_own, scores[0], scores[reach])] + scores[1:reach]
        peak = jnp.max(functools.reduce(jnp.maximum, scores), axis=1, keepdims=True)
        expo = [jnp.exp2((x - peak) * factor) for x in scores]
        expo = (
            [jnp.where(is_own, expo[0], 0.0)] + expo[1:] + [jnp.where(is_own, 0.0, expo[0])]
        )
        update = functools.reduce(
            jnp.add,
            [
                dot(x.astype(jnp.bfloat16), jnp.concatenate([kv[d, g, :, HD : 2 * HD], ones], axis=1))
                for d, x in enumerate(expo)
            ],
        )
        attn = (update[:, 0:HD] / update[:, HD : 2 * HD]).astype(jnp.bfloat16)
        for k in range(TOGETHER):
            sendb[to, :, pl.ds(pl.multiple_of((h + k - to * cut_heads) * HD, HD), HD)] = attn[
                k * rows : (k + 1) * rows
            ]

    for c in range(cuts):
        g = c * cut_heads // per_shared
        if c * cut_heads % per_shared == 0:
            for e in range(1, reach):

                @pl.when(s >= e)
                def _():
                    near_copy(g, e, 0).wait_recv()

        def heads(i):
            w_step = PIECES * TOGETHER // (cuts * cut_heads)
            first = (c * cut_heads // TOGETHER + i) * w_step
            loop(first, first + w_step, lambda j: w_copy(j).start())
            some_heads(g, c * cut_heads + i * TOGETHER, c)

        loop(0, cut_heads // TOGETHER, heads)
        loop(1, n, lambda e: a2a_copy(c, e).start())
        keep = pl.ds(pl.multiple_of(s * per_pair, per_pair), per_pair)
        arr[c, keep, :] = sendb[c, keep, :]

    def wide_cut(c):
        return pl.ds(pl.multiple_of(c * WIDE, WIDE), WIDE)

    def sum_copy(c):
        return pltpu.make_async_remote_copy(
            src_ref=part.at[c, other_half], dst_ref=other.at[c],
            send_sem=sum_send.at[c], recv_sem=sum_recv.at[c],
            device_id={"tp": 1 - t}, device_id_type=MESH,
        )

    def keep_copy(c):
        return pltpu.make_async_copy(part.at[c, own_half], out_ref.at[:, wide_cut(c)], keep_sem.at[c])

    def finish(c):
        sum_copy(c).wait_recv()
        total = part[c, own_half, :].astype(jnp.float32) + other[c].astype(jnp.float32)
        part[c, own_half, :] = total.astype(jnp.bfloat16)
        keep_copy(c).start()

    for first, last in ((0, cuts - 1), (cuts - 1, cuts)):
        share = PIECES // cuts
        loop(first * share, last * share, lambda i: w_copy(i).wait())
        for c in range(first, last):
            loop(1, n, lambda e: a2a_copy(c, e).wait_recv())
            mixed[:, c * depth : (c + 1) * depth] = dot(recv_perm[...], arr[c]).astype(jnp.bfloat16)
        deep = slice(first * depth, last * depth)

        def one_width(c):
            term = dot(mixed[:, deep], wbuf[deep, wide_cut(c)])
            if last < cuts:
                acc[c] = term
            else:
                part[c] = (acc[c] + term).astype(jnp.bfloat16)
                sum_copy(c).start()

                @pl.when(c >= BEHIND)
                def _():
                    finish(c - BEHIND)

        loop(0, wide_count, one_width)

    loop(wide_count - BEHIND, wide_count, finish)
    loop(0, wide_count, lambda c: keep_copy(c).wait())

    for g in range(shared):
        pair_copy(g).wait_send()

        @pl.when(s + reach < n)
        def _():
            far_copy(g).wait_send()

        for e in range(1, reach):

            @pl.when((place + e < reach) | (s >= reach))
            def _():
                near_copy(g, e, 0).wait_send()

    for c in range(cuts):
        loop(1, n, lambda e: a2a_copy(c, e).wait_send())
    loop(0, wide_count, lambda c: sum_copy(c).wait_send())


def copy_kernel(from_ref, to_ref, held, in_sem, out_sem):
    rows = from_ref.shape[0] // COPIES

    def cut(i):
        return pl.ds(i * rows, rows)

    def take(i):
        return pltpu.make_async_copy(from_ref.at[cut(i)], held.at[cut(i)], in_sem.at[i])

    def give(i):
        return pltpu.make_async_copy(held.at[cut(i)], to_ref.at[cut(i)], out_sem.at[i])

    for i in range(COPIES):
        take(i).start()
    for i in range(COPIES):
        take(i).wait()
        give(i).start()
    for i in range(COPIES):
        give(i).wait()


def fused_shards(segment_ids, relayout, queries, keys, values, out_weight):
    n = lax.axis_size("seq")
    rows = queries.shape[0]
    reach = n // LONGEST_SHARE
    shared = keys.shape[1] // HD // 2
    depth = queries.shape[1] // CUTS
    width = out_weight.shape[1]
    wide_count = width // WIDE
    bf16, f32 = jnp.bfloat16, jnp.float32
    dma = pltpu.SemaphoreType.DMA
    vmem = pl.BlockSpec(memory_space=pltpu.VMEM)
    result = pl.pallas_call(
        functools.partial(fused_kernel, n, reach),
        out_shape=jax.ShapeDtypeStruct((rows // 2, width), bf16),
        in_specs=[vmem] * 5 + [pl.BlockSpec(memory_space=pl.ANY)],
        out_specs=pl.BlockSpec(memory_space=pl.ANY),
        scratch_shapes=[
            pltpu.VMEM((n, rows), jnp.int32),
            pltpu.VMEM((n, rows), jnp.int32),
            pltpu.VMEM((reach + 1, shared, rows, 2 * HD), bf16),
            pltpu.VMEM((shared, rows // 2, 2 * HD), bf16),
            pltpu.VMEM((reach + 1, rows, HD), bf16),
            pltpu.VMEM((rows, HD), bf16),
            pltpu.VMEM((rows, rows), f32),
            pltpu.VMEM((rows, rows), bf16),
            pltpu.VMEM((rows, rows), bf16),
            pltpu.VMEM((n, rows), f32),
            pltpu.VMEM(queries.shape, bf16),
            pltpu.VMEM(queries.shape, bf16),
            pltpu.VMEM((CUTS, rows, depth), bf16),
            pltpu.VMEM((CUTS, rows, depth), bf16),
            pltpu.VMEM((wide_count, rows, WIDE), f32),
            pltpu.VMEM((wide_count, rows, WIDE), bf16),
            pltpu.VMEM((wide_count, rows // 2, WIDE), bf16),
            pltpu.VMEM(out_weight.shape, bf16),
            dma((PIECES,)),
            dma((shared,)),
            dma((shared,)),
            dma((shared,)),
            dma((shared,)),
            dma((shared, reach)),
            dma((shared, reach)),
            dma((CUTS, n)),
            dma((CUTS, n)),
            dma((wide_count,)),
            dma((wide_count,)),
            dma((wide_count,)),
        ],
        compiler_params=pltpu.CompilerParams(
            collective_id=0, has_side_effects=True, vmem_limit_bytes=63 * 1024 * 1024
        ),
    )(segment_ids.reshape(-1, 128), relayout.reshape(-1, 128), queries, keys, values, out_weight)
    return pl.pallas_call(
        copy_kernel,
        out_shape=jax.ShapeDtypeStruct(result.shape, bf16),
        in_specs=[pl.BlockSpec(memory_space=pl.ANY)],
        out_specs=pl.BlockSpec(memory_space=pl.ANY),
        scratch_shapes=[pltpu.VMEM(result.shape, bf16), dma((COPIES,)), dma((COPIES,))],
    )(result)


def shards(segment_ids, relayout, queries, keys, values, out_weight):
    rows_here = queries.shape[0]
    seq_count = lax.axis_size("seq")
    seq_index = lax.axis_index("seq")
    tp_index = lax.axis_index("tp")
    total_rows = rows_here * seq_count
    heads_here = queries.shape[1] // HD
    group = QH // KVH
    shared_here = max(1, heads_here // group)
    per_shared = heads_here // shared_here
    scale = HD ** (-0.5)
    all_keys, all_values = (
        lax.all_gather(keys, "tp", axis=0, tiled=True),
        lax.all_gather(values, "tp", axis=0, tiled=True),
    )
    first_head = tp_index * heads_here // group
    own_keys = lax.dynamic_slice_in_dim(all_keys, first_head * HD, shared_here * HD, 1)
    own_values = lax.dynamic_slice_in_dim(all_values, first_head * HD, shared_here * HD, 1)
    own_pair = jnp.stack([own_keys, own_values])
    row_ids = jnp.arange(rows_here, dtype=jnp.int32)
    inverse = (
        jnp.zeros((total_rows,), jnp.int32)
        .at[relayout]
        .set(jnp.arange(total_rows, dtype=jnp.int32))
    )
    new_here = seq_index * rows_here + row_ids
    old_here = seq_index * rows_here + row_ids
    source_block = relayout[new_here] // rows_here
    arrival = jnp.argsort(source_block * total_rows + new_here)
    send_order = jnp.argsort(inverse[old_here])
    arrived = lax.all_to_all(queries[send_order], "seq", split_axis=0, concat_axis=0, tiled=True)
    query_pos = relayout[seq_index * rows_here + arrival]
    query_seg = segment_ids[query_pos]
    pieces = lax.all_gather(own_pair, "seq", axis=1, tiled=True)
    count = pieces.shape[1]
    key_pos = jnp.arange(count, dtype=jnp.int32)
    live = (
        (key_pos[None, :] <= query_pos[:, None])
        & (segment_ids[None, :] == query_seg[:, None])
        & (jnp.int32(0) >= 0)
    )
    query_split = arrived.reshape(rows_here, shared_here, per_shared, HD)
    key_split = pieces[0].reshape(count, shared_here, HD)
    value_split = pieces[1].reshape(count, shared_here, HD)
    scores = (
        jnp.einsum("qngd,knd->ngqk", query_split, key_split, preferred_element_type=jnp.float32)
        * scale
    )
    masked = jnp.where(live, scores, jnp.float32(-1e30))
    peak = jnp.full((shared_here, per_shared, rows_here), -1e30, jnp.float32)
    new_peak = jnp.maximum(peak, jnp.max(masked, axis=-1))
    expo = jnp.where(live, jnp.exp(masked - new_peak[..., None]), jnp.float32(0.0))
    denom = jnp.sum(expo, axis=-1)
    update = jnp.einsum(
        "ngqk,knd->ngqd", expo.astype(jnp.bfloat16), value_split, preferred_element_type=jnp.float32
    )
    attn = update / denom[..., None]
    attn_rows = (
        jnp.transpose(attn, (2, 0, 1, 3)).reshape(rows_here, heads_here * HD).astype(jnp.bfloat16)
    )
    attn_new = jnp.zeros_like(attn_rows).at[arrival].set(attn_rows)
    return lax.psum_scatter(
        jnp.dot(attn_new, out_weight, preferred_element_type=jnp.float32).astype(jnp.bfloat16),
        "tp",
        scatter_dimension=0,
        tiled=True,
    )


def solution(mesh):
    return jax.shard_map(
        fused_shards if mesh.shape["tp"] == 2 else shards,
        mesh=mesh,
        in_specs=(
            P(),
            P(),
            P("seq", "tp"),
            P(("seq", "tp"), None),
            P(("seq", "tp"), None),
            P("tp", None),
        ),
        out_specs=P(("seq", "tp"), None),
        check_vma=False,
    )
```

```python
import functools

import jax
import jax.numpy as jnp
from jax import lax
from jax.experimental import pallas as pl
from jax.experimental.pallas import tpu as pltpu
from jax.sharding import PartitionSpec as P

QH = 32
KVH = 4
HD = 128
LONGEST_SHARE = 4
MESH = pl.DeviceIdType.MESH
WIDE = 512
PIECES = 32
CUTS = 4
TOGETHER = 2
BEHIND = 8
COPIES = 8
SPREAD = 7


def dot(a, b):
    return jnp.dot(a, b, preferred_element_type=jnp.float32)


def dot_nt(a, b):
    return lax.dot_general(a, b, (((1,), (1,)), ((), ())), preferred_element_type=jnp.float32)


def loop(low, high, body):
    def step(i, carry):
        body(i)
        return carry

    lax.fori_loop(low, high, step, 0)


def fused_kernel(
    n, reach, seg_in, lay_in, q_ref, k_ref, v_ref, w_hbm, out_ref,
    seg_ref, lay_ref, kv, stage, key_tag, query_tag, own_first, send_perm, recv_perm, rank_ref, q_sorted,
    mixed, sendb, arr, acc, part, other, wbuf,
    w_sem, pair_send, pair_recv, far_send, far_recv, near_send, near_recv,
    a2a_send, a2a_recv, sum_send, sum_recv, keep_sem,
):
    s = lax.axis_index("seq")
    t = lax.axis_index("tp")
    rows = q_ref.shape[0]
    half = rows // 2
    per_pair = rows // n
    shared = kv.shape[1]
    per_shared = q_ref.shape[1] // HD // shared
    cuts, _, depth = sendb.shape
    cut_heads = depth // HD
    wide_count = acc.shape[0]
    w_rows = w_hbm.shape[0] // PIECES
    place = lax.rem(s, reach)
    base = s - place

    barrier = pltpu.get_barrier_semaphore()
    loop(
        1, n,
        lambda e: pl.semaphore_signal(
            barrier, inc=1, device_id={"seq": lax.rem(s + e, n)}, device_id_type=MESH
        ),
    )
    pl.semaphore_signal(barrier, inc=1, device_id={"tp": 1 - t}, device_id_type=MESH)

    def w_copy(i):
        cut = pl.ds(pl.multiple_of(i * w_rows, w_rows), w_rows)
        return pltpu.make_async_copy(w_hbm.at[cut], wbuf.at[cut], w_sem.at[i])

    own_half = pl.ds(pl.multiple_of(t * half, half), half)
    other_half = pl.ds(pl.multiple_of((1 - t) * half, half), half)
    for g in range(shared):
        mine = pl.ds(pl.multiple_of((t * shared + g) * HD, HD), HD)
        theirs = pl.ds(pl.multiple_of(((1 - t) * shared + g) * HD, HD), HD)
        kv[0, g, own_half, 0:HD] = k_ref[:, mine]
        kv[0, g, own_half, HD : 2 * HD] = v_ref[:, mine]
        stage[g, :, 0:HD] = k_ref[:, theirs]
        stage[g, :, HD : 2 * HD] = v_ref[:, theirs]

    pl.semaphore_wait(barrier, n)

    def pair_copy(g):
        return pltpu.make_async_remote_copy(
            src_ref=stage.at[g], dst_ref=kv.at[0, g, own_half],
            send_sem=pair_send.at[g], recv_sem=pair_recv.at[g],
            device_id={"tp": 1 - t}, device_id_type=MESH,
        )

    def far_copy(g):
        return pltpu.make_async_remote_copy(
            src_ref=kv.at[0, g], dst_ref=kv.at[reach, g],
            send_sem=far_send.at[g], recv_sem=far_recv.at[g],
            device_id={"seq": lax.rem(s + reach, n)}, device_id_type=MESH,
        )

    def near_copy(g, e, slot):
        return pltpu.make_async_remote_copy(
            src_ref=kv.at[slot, g], dst_ref=kv.at[e, g],
            send_sem=near_send.at[g, e], recv_sem=near_recv.at[g, e],
            device_id={"seq": base + lax.rem(place + e, reach)}, device_id_type=MESH,
        )

    def own_out(g):
        pair_copy(g).wait_recv()

        @pl.when(s + reach < n)
        def _():
            far_copy(g).start()

        for e in range(1, reach):

            @pl.when(place + e < reach)
            def _():
                near_copy(g, e, 0).start()

    def relay(g):
        @pl.when(s >= reach)
        def _():
            far_copy(g).wait_recv()
            for e in range(1, reach):

                @pl.when(place + e >= reach)
                def _():
                    near_copy(g, e, reach).start()

    for g in range(shared):
        pair_copy(g).start()
    for e in range(1, reach + 1):

        @pl.when(s < e)
        def _():
            kv[e] = jnp.zeros_like(kv[e])

    own_out(0)

    lines = rows // 128
    for ref, source in ((seg_ref, seg_in), (lay_ref, lay_in)):
        for i in range(lines):
            ref[:, i * 128 : (i + 1) * 128] = source[pl.ds(i, n, stride=lines), :]

    tag_id = lax.broadcasted_iota(jnp.int32, (rows, HD), 1)
    for d in range(reach + 1):
        key_seg = jnp.where(s >= d, seg_ref[pl.ds(jnp.maximum(s - d, 0), 1), :], HD - 1)
        key_col = jnp.broadcast_to(key_seg, (HD, rows)).T
        key_tag[d] = jnp.where(key_col == tag_id, 1.0, 0.0).astype(jnp.bfloat16)

    relay(0)
    for g in range(1, shared):
        own_out(g)

    row_id = lax.broadcasted_iota(jnp.int32, (rows, rows), 0)
    col_id = lax.broadcasted_iota(jnp.int32, (rows, rows), 1)

    before = jnp.where(row_id < col_id, 1.0, 0.0).astype(jnp.bfloat16)
    local = lay_ref[...] - s * rows
    is_mine = (local >= 0) & (local < rows)
    ranks = dot(jnp.where(is_mine, 1.0, 0.0).astype(jnp.bfloat16), before)
    rank_ref[...] = jnp.where(is_mine, ranks, -1.0)
    rank_id = lax.broadcasted_iota(jnp.int32, (per_pair, rows), 0).astype(jnp.float32)

    def one_target(b):
        pick = jnp.where(rank_ref[pl.ds(b, 1), :] == rank_id, 1.0, 0.0).astype(jnp.bfloat16)
        token = jnp.where(lay_ref[pl.ds(b, 1), :] - s * rows == row_id, 1.0, 0.0).astype(jnp.bfloat16)
        cut = pl.ds(pl.multiple_of(b * per_pair, per_pair), per_pair)
        send_perm[cut, :] = dot_nt(pick, token).astype(jnp.bfloat16)

    loop(0, n, one_target)

    def sort_queries(c):
        cut = pl.ds(pl.multiple_of(c * depth, depth), depth)
        q_sorted[:, cut] = dot(send_perm[...], q_ref[:, cut]).astype(jnp.bfloat16)

    loop(0, cuts, sort_queries)
    chosen = send_perm[...].astype(jnp.float32)
    position = jnp.sum(chosen * col_id.astype(jnp.float32), axis=1, keepdims=True)
    document = jnp.sum(chosen * seg_ref[pl.ds(s, 1), :].astype(jnp.float32), axis=1, keepdims=True)
    query_tag[...] = jnp.where(document == tag_id.astype(jnp.float32), 0.0, -1e30).astype(jnp.bfloat16)
    own_first[...] = jnp.where(col_id.astype(jnp.float32) <= position, 1.0, 0.0)

    origin = lay_ref[pl.ds(s, 1), :] // rows
    block_id = lax.broadcasted_iota(jnp.int32, (n, rows), 0)
    from_block = jnp.where(origin == block_id, 1.0, 0.0)
    earlier = dot(from_block.astype(jnp.bfloat16), before)
    rank = jnp.sum(from_block * earlier, axis=0, keepdims=True)
    slot_of = origin.astype(jnp.float32) * per_pair + rank
    slot_col = jnp.broadcast_to(slot_of, (rows, rows)).T
    recv_perm[...] = jnp.where(slot_col == col_id.astype(jnp.float32), 1.0, 0.0).astype(jnp.bfloat16)

    for g in range(1, shared):
        relay(g)

    def a2a_copy(g, e):
        target = lax.rem(s + SPREAD * e, n)
        return pltpu.make_async_remote_copy(
            src_ref=sendb.at[g, pl.ds(pl.multiple_of(target * per_pair, per_pair), per_pair)],
            dst_ref=arr.at[g, pl.ds(pl.multiple_of(s * per_pair, per_pair), per_pair)],
            send_sem=a2a_send.at[g, e], recv_sem=a2a_recv.at[g, e],
            device_id={"seq": target}, device_id_type=MESH,
        )

    factor = HD ** (-0.5) * 1.4426950408889634

    all_ones = jnp.ones(((reach + 1) * rows, HD), jnp.bfloat16)

    def one_head(g, h, to):
        q = q_sorted[:, pl.ds(pl.multiple_of(h * HD, HD), HD)]
        q = jnp.concatenate([q, query_tag[...]], axis=1)
        scores = [
            dot_nt(q, jnp.concatenate([kv[d, g, :, 0:HD], key_tag[d]], axis=1)) for d in range(reach + 1)
        ]
        is_own = own_first[...] > 0.5
        scores = [jnp.where(is_own, scores[0], scores[reach])] + scores[1:reach]
        peak = jnp.max(functools.reduce(jnp.maximum, scores), axis=1, keepdims=True)
        expo = [jnp.exp2((x - peak) * factor) for x in scores]
        expo = (
            [jnp.where(is_own, expo[0], 0.0)] + expo[1:] + [jnp.where(is_own, 0.0, expo[0])]
        )
        weight = jnp.concatenate([x.astype(jnp.bfloat16) for x in expo], axis=1)
        value = jnp.concatenate([kv[d, g, :, HD : 2 * HD] for d in range(reach + 1)], axis=0)
        update = dot(weight, jnp.concatenate([value, all_ones], axis=1))
        sendb[to, :, pl.ds(pl.multiple_of((h - to * cut_heads) * HD, HD), HD)] = (
            update[:, 0:HD] / update[:, HD : 2 * HD]
        ).astype(jnp.bfloat16)

    for c in range(cuts):
        g = c * cut_heads // per_shared
        if c * cut_heads % per_shared == 0:
            for e in range(1, reach):

                @pl.when(s >= e)
                def _():
                    near_copy(g, e, 0).wait_recv()

        def heads(i):
            w_step = PIECES * TOGETHER // (cuts * cut_heads)
            first = (c * cut_heads // TOGETHER + i) * w_step
            loop(first, first + w_step, lambda j: w_copy(j).start())
            for k in range(TOGETHER):
                one_head(g, c * cut_heads + i * TOGETHER + k, c)

        loop(0, cut_heads // TOGETHER, heads)
        loop(1, n, lambda e: a2a_copy(c, e).start())
        keep = pl.ds(pl.multiple_of(s * per_pair, per_pair), per_pair)
        arr[c, keep, :] = sendb[c, keep, :]

    def wide_cut(c):
        return pl.ds(pl.multiple_of(c * WIDE, WIDE), WIDE)

    def sum_copy(c):
        return pltpu.make_async_remote_copy(
            src_ref=part.at[c, other_half], dst_ref=other.at[c],
            send_sem=sum_send.at[c], recv_sem=sum_recv.at[c],
            device_id={"tp": 1 - t}, device_id_type=MESH,
        )

    def keep_copy(c):
        return pltpu.make_async_copy(part.at[c, own_half], out_ref.at[:, wide_cut(c)], keep_sem.at[c])

    def finish(c):
        sum_copy(c).wait_recv()
        total = part[c, own_half, :].astype(jnp.float32) + other[c].astype(jnp.float32)
        part[c, own_half, :] = total.astype(jnp.bfloat16)
        keep_copy(c).start()

    for g in range(cuts):
        share = PIECES // cuts
        loop(g * share, (g + 1) * share, lambda i: w_copy(i).wait())
        loop(1, n, lambda e: a2a_copy(g, e).wait_recv())
        mixed[...] = dot(recv_perm[...], arr[g]).astype(jnp.bfloat16)

        def one_width(c):
            term = dot(mixed[...], wbuf[g * depth : (g + 1) * depth, wide_cut(c)])
            if g > 0:
                term = term + acc[c]
            if g < cuts - 1:
                acc[c] = term
            else:
                part[c] = term.astype(jnp.bfloat16)
                sum_copy(c).start()

                @pl.when(c >= BEHIND)
                def _():
                    finish(c - BEHIND)

        loop(0, wide_count, one_width)

    loop(wide_count - BEHIND, wide_count, finish)
    loop(0, wide_count, lambda c: keep_copy(c).wait())

    for g in range(shared):
        pair_copy(g).wait_send()

        @pl.when(s + reach < n)
        def _():
            far_copy(g).wait_send()

        for e in range(1, reach):

            @pl.when((place + e < reach) | (s >= reach))
            def _():
                near_copy(g, e, 0).wait_send()

    for c in range(cuts):
        loop(1, n, lambda e: a2a_copy(c, e).wait_send())
    loop(0, wide_count, lambda c: sum_copy(c).wait_send())


def copy_kernel(from_ref, to_ref, held, in_sem, out_sem):
    rows = from_ref.shape[0] // COPIES

    def cut(i):
        return pl.ds(i * rows, rows)

    def take(i):
        return pltpu.make_async_copy(from_ref.at[cut(i)], held.at[cut(i)], in_sem.at[i])

    def give(i):
        return pltpu.make_async_copy(held.at[cut(i)], to_ref.at[cut(i)], out_sem.at[i])

    for i in range(COPIES):
        take(i).start()
    for i in range(COPIES):
        take(i).wait()
        give(i).start()
    for i in range(COPIES):
        give(i).wait()


def fused_shards(segment_ids, relayout, queries, keys, values, out_weight):
    n = lax.axis_size("seq")
    rows = queries.shape[0]
    reach = n // LONGEST_SHARE
    shared = keys.shape[1] // HD // 2
    depth = queries.shape[1] // CUTS
    width = out_weight.shape[1]
    wide_count = width // WIDE
    bf16, f32 = jnp.bfloat16, jnp.float32
    dma = pltpu.SemaphoreType.DMA
    vmem = pl.BlockSpec(memory_space=pltpu.VMEM)
    result = pl.pallas_call(
        functools.partial(fused_kernel, n, reach),
        out_shape=jax.ShapeDtypeStruct((rows // 2, width), bf16),
        in_specs=[vmem] * 5 + [pl.BlockSpec(memory_space=pl.ANY)],
        out_specs=pl.BlockSpec(memory_space=pl.ANY),
        scratch_shapes=[
            pltpu.VMEM((n, rows), jnp.int32),
            pltpu.VMEM((n, rows), jnp.int32),
            pltpu.VMEM((reach + 1, shared, rows, 2 * HD), bf16),
            pltpu.VMEM((shared, rows // 2, 2 * HD), bf16),
            pltpu.VMEM((reach + 1, rows, HD), bf16),
            pltpu.VMEM((rows, HD), bf16),
            pltpu.VMEM((rows, rows), f32),
            pltpu.VMEM((rows, rows), bf16),
            pltpu.VMEM((rows, rows), bf16),
            pltpu.VMEM((n, rows), f32),
            pltpu.VMEM(queries.shape, bf16),
            pltpu.VMEM((rows, depth), bf16),
            pltpu.VMEM((CUTS, rows, depth), bf16),
            pltpu.VMEM((CUTS, rows, depth), bf16),
            pltpu.VMEM((wide_count, rows, WIDE), f32),
            pltpu.VMEM((wide_count, rows, WIDE), bf16),
            pltpu.VMEM((wide_count, rows // 2, WIDE), bf16),
            pltpu.VMEM(out_weight.shape, bf16),
            dma((PIECES,)),
            dma((shared,)),
            dma((shared,)),
            dma((shared,)),
            dma((shared,)),
            dma((shared, reach)),
            dma((shared, reach)),
            dma((CUTS, n)),
            dma((CUTS, n)),
            dma((wide_count,)),
            dma((wide_count,)),
            dma((wide_count,)),
        ],
        compiler_params=pltpu.CompilerParams(
            collective_id=0, has_side_effects=True, vmem_limit_bytes=63 * 1024 * 1024
        ),
    )(segment_ids.reshape(-1, 128), relayout.reshape(-1, 128), queries, keys, values, out_weight)
    return pl.pallas_call(
        copy_kernel,
        out_shape=jax.ShapeDtypeStruct(result.shape, bf16),
        in_specs=[pl.BlockSpec(memory_space=pl.ANY)],
        out_specs=pl.BlockSpec(memory_space=pl.ANY),
        scratch_shapes=[pltpu.VMEM(result.shape, bf16), dma((COPIES,)), dma((COPIES,))],
    )(result)


def shards(segment_ids, relayout, queries, keys, values, out_weight):
    rows_here = queries.shape[0]
    seq_count = lax.axis_size("seq")
    seq_index = lax.axis_index("seq")
    tp_index = lax.axis_index("tp")
    total_rows = rows_here * seq_count
    heads_here = queries.shape[1] // HD
    group = QH // KVH
    shared_here = max(1, heads_here // group)
    per_shared = heads_here // shared_here
    scale = HD ** (-0.5)
    all_keys, all_values = (
        lax.all_gather(keys, "tp", axis=0, tiled=True),
        lax.all_gather(values, "tp", axis=0, tiled=True),
    )
    first_head = tp_index * heads_here // group
    own_keys = lax.dynamic_slice_in_dim(all_keys, first_head * HD, shared_here * HD, 1)
    own_values = lax.dynamic_slice_in_dim(all_values, first_head * HD, shared_here * HD, 1)
    own_pair = jnp.stack([own_keys, own_values])
    row_ids = jnp.arange(rows_here, dtype=jnp.int32)
    inverse = (
        jnp.zeros((total_rows,), jnp.int32)
        .at[relayout]
        .set(jnp.arange(total_rows, dtype=jnp.int32))
    )
    new_here = seq_index * rows_here + row_ids
    old_here = seq_index * rows_here + row_ids
    source_block = relayout[new_here] // rows_here
    arrival = jnp.argsort(source_block * total_rows + new_here)
    send_order = jnp.argsort(inverse[old_here])
    arrived = lax.all_to_all(queries[send_order], "seq", split_axis=0, concat_axis=0, tiled=True)
    query_pos = relayout[seq_index * rows_here + arrival]
    query_seg = segment_ids[query_pos]
    pieces = lax.all_gather(own_pair, "seq", axis=1, tiled=True)
    count = pieces.shape[1]
    key_pos = jnp.arange(count, dtype=jnp.int32)
    live = (
        (key_pos[None, :] <= query_pos[:, None])
        & (segment_ids[None, :] == query_seg[:, None])
        & (jnp.int32(0) >= 0)
    )
    query_split = arrived.reshape(rows_here, shared_here, per_shared, HD)
    key_split = pieces[0].reshape(count, shared_here, HD)
    value_split = pieces[1].reshape(count, shared_here, HD)
    scores = (
        jnp.einsum("qngd,knd->ngqk", query_split, key_split, preferred_element_type=jnp.float32)
        * scale
    )
    masked = jnp.where(live, scores, jnp.float32(-1e30))
    peak = jnp.full((shared_here, per_shared, rows_here), -1e30, jnp.float32)
    new_peak = jnp.maximum(peak, jnp.max(masked, axis=-1))
    expo = jnp.where(live, jnp.exp(masked - new_peak[..., None]), jnp.float32(0.0))
    denom = jnp.sum(expo, axis=-1)
    update = jnp.einsum(
        "ngqk,knd->ngqd", expo.astype(jnp.bfloat16), value_split, preferred_element_type=jnp.float32
    )
    attn = update / denom[..., None]
    attn_rows = (
        jnp.transpose(attn, (2, 0, 1, 3)).reshape(rows_here, heads_here * HD).astype(jnp.bfloat16)
    )
    attn_new = jnp.zeros_like(attn_rows).at[arrival].set(attn_rows)
    return lax.psum_scatter(
        jnp.dot(attn_new, out_weight, preferred_element_type=jnp.float32).astype(jnp.bfloat16),
        "tp",
        scatter_dimension=0,
        tiled=True,
    )


def solution(mesh):
    return jax.shard_map(
        fused_shards if mesh.shape["tp"] == 2 else shards,
        mesh=mesh,
        in_specs=(
            P(),
            P(),
            P("seq", "tp"),
            P(("seq", "tp"), None),
            P(("seq", "tp"), None),
            P("tp", None),
        ),
        out_specs=P(("seq", "tp"), None),
        check_vma=False,
    )
```

```python
import functools

import jax
import jax.numpy as jnp
from jax import lax
from jax.experimental import pallas as pl
from jax.experimental.pallas import tpu as pltpu
from jax.sharding import PartitionSpec as P

QH = 32
KVH = 4
HD = 128
LONGEST_SHARE = 4
MESH = pl.DeviceIdType.MESH
WIDE = 512
PIECES = 32
CUTS = 4
TOGETHER = 2
BEHIND = 8
COPIES = 8


def dot(a, b):
    return jnp.dot(a, b, preferred_element_type=jnp.float32)


def dot_nt(a, b):
    return lax.dot_general(a, b, (((1,), (1,)), ((), ())), preferred_element_type=jnp.float32)


def loop(low, high, body):
    def step(i, carry):
        body(i)
        return carry

    lax.fori_loop(low, high, step, 0)


def fused_kernel(
    n, reach, seg_in, lay_in, q_ref, k_ref, v_ref, w_hbm, out_ref,
    seg_ref, lay_ref, kv, stage, key_tag, query_tag, own_first, send_perm, recv_perm, rank_ref, q_sorted,
    mixed, sendb, passed, arr, acc, part, other, wbuf,
    w_sem, pair_send, pair_recv, far_send, far_recv, near_send, near_recv,
    deal_send, deal_recv, pass_send, pass_recv, sum_send, sum_recv, keep_sem,
):
    s = lax.axis_index("seq")
    t = lax.axis_index("tp")
    rows = q_ref.shape[0]
    half = rows // 2
    per_pair = rows // n
    shared = kv.shape[1]
    per_shared = q_ref.shape[1] // HD // shared
    cuts, _, depth = sendb.shape
    cut_heads = depth // HD
    wide_count = acc.shape[0]
    w_rows = w_hbm.shape[0] // PIECES
    place = lax.rem(s, reach)
    base = s - place

    barrier = pltpu.get_barrier_semaphore()
    loop(
        1, n,
        lambda e: pl.semaphore_signal(
            barrier, inc=1, device_id={"seq": lax.rem(s + e, n)}, device_id_type=MESH
        ),
    )
    pl.semaphore_signal(barrier, inc=1, device_id={"tp": 1 - t}, device_id_type=MESH)

    def w_copy(i):
        cut = pl.ds(pl.multiple_of(i * w_rows, w_rows), w_rows)
        return pltpu.make_async_copy(w_hbm.at[cut], wbuf.at[cut], w_sem.at[i])

    own_half = pl.ds(pl.multiple_of(t * half, half), half)
    other_half = pl.ds(pl.multiple_of((1 - t) * half, half), half)
    for g in range(shared):
        mine = pl.ds(pl.multiple_of((t * shared + g) * HD, HD), HD)
        theirs = pl.ds(pl.multiple_of(((1 - t) * shared + g) * HD, HD), HD)
        kv[0, g, own_half, 0:HD] = k_ref[:, mine]
        kv[0, g, own_half, HD : 2 * HD] = v_ref[:, mine]
        stage[g, :, 0:HD] = k_ref[:, theirs]
        stage[g, :, HD : 2 * HD] = v_ref[:, theirs]

    pl.semaphore_wait(barrier, n)

    def pair_copy(g):
        return pltpu.make_async_remote_copy(
            src_ref=stage.at[g], dst_ref=kv.at[0, g, own_half],
            send_sem=pair_send.at[g], recv_sem=pair_recv.at[g],
            device_id={"tp": 1 - t}, device_id_type=MESH,
        )

    def far_copy(g):
        return pltpu.make_async_remote_copy(
            src_ref=kv.at[0, g], dst_ref=kv.at[reach, g],
            send_sem=far_send.at[g], recv_sem=far_recv.at[g],
            device_id={"seq": lax.rem(s + reach, n)}, device_id_type=MESH,
        )

    def near_copy(g, e, slot):
        return pltpu.make_async_remote_copy(
            src_ref=kv.at[slot, g], dst_ref=kv.at[e, g],
            send_sem=near_send.at[g, e], recv_sem=near_recv.at[g, e],
            device_id={"seq": base + lax.rem(place + e, reach)}, device_id_type=MESH,
        )

    def own_out(g):
        pair_copy(g).wait_recv()

        @pl.when(s + reach < n)
        def _():
            far_copy(g).start()

        for e in range(1, reach):

            @pl.when(place + e < reach)
            def _():
                near_copy(g, e, 0).start()

    def relay(g):
        @pl.when(s >= reach)
        def _():
            far_copy(g).wait_recv()
            for e in range(1, reach):

                @pl.when(place + e >= reach)
                def _():
                    near_copy(g, e, reach).start()

    for g in range(shared):
        pair_copy(g).start()
    for e in range(1, reach + 1):

        @pl.when(s < e)
        def _():
            kv[e] = jnp.zeros_like(kv[e])

    own_out(0)

    lines = rows // 128
    for ref, source in ((seg_ref, seg_in), (lay_ref, lay_in)):
        for i in range(lines):
            ref[:, i * 128 : (i + 1) * 128] = source[pl.ds(i, n, stride=lines), :]

    tag_id = lax.broadcasted_iota(jnp.int32, (rows, HD), 1)
    for d in range(reach + 1):
        key_seg = jnp.where(s >= d, seg_ref[pl.ds(jnp.maximum(s - d, 0), 1), :], HD - 1)
        key_col = jnp.broadcast_to(key_seg, (HD, rows)).T
        key_tag[d] = jnp.where(key_col == tag_id, 1.0, 0.0).astype(jnp.bfloat16)

    relay(0)
    for g in range(1, shared):
        own_out(g)

    row_id = lax.broadcasted_iota(jnp.int32, (rows, rows), 0)
    col_id = lax.broadcasted_iota(jnp.int32, (rows, rows), 1)

    before = jnp.where(row_id < col_id, 1.0, 0.0).astype(jnp.bfloat16)
    local = lay_ref[...] - s * rows
    is_mine = (local >= 0) & (local < rows)
    ranks = dot(jnp.where(is_mine, 1.0, 0.0).astype(jnp.bfloat16), before)
    rank_ref[...] = jnp.where(is_mine, ranks, -1.0)
    rank_id = lax.broadcasted_iota(jnp.int32, (per_pair, rows), 0).astype(jnp.float32)

    def one_target(b):
        pick = jnp.where(rank_ref[pl.ds(b, 1), :] == rank_id, 1.0, 0.0).astype(jnp.bfloat16)
        token = jnp.where(lay_ref[pl.ds(b, 1), :] - s * rows == row_id, 1.0, 0.0).astype(jnp.bfloat16)
        cut = pl.ds(pl.multiple_of(b * per_pair, per_pair), per_pair)
        send_perm[cut, :] = dot_nt(pick, token).astype(jnp.bfloat16)

    loop(0, n, one_target)

    def sort_queries(c):
        cut = pl.ds(pl.multiple_of(c * depth, depth), depth)
        q_sorted[:, cut] = dot(send_perm[...], q_ref[:, cut]).astype(jnp.bfloat16)

    loop(0, cuts, sort_queries)
    chosen = send_perm[...].astype(jnp.float32)
    position = jnp.sum(chosen * col_id.astype(jnp.float32), axis=1, keepdims=True)
    document = jnp.sum(chosen * seg_ref[pl.ds(s, 1), :].astype(jnp.float32), axis=1, keepdims=True)
    query_tag[...] = jnp.where(document == tag_id.astype(jnp.float32), 0.0, -1e30).astype(jnp.bfloat16)
    own_first[...] = jnp.where(col_id.astype(jnp.float32) <= position, 1.0, 0.0)

    origin = lay_ref[pl.ds(s, 1), :] // rows
    block_id = lax.broadcasted_iota(jnp.int32, (n, rows), 0)
    from_block = jnp.where(origin == block_id, 1.0, 0.0)
    earlier = dot(from_block.astype(jnp.bfloat16), before)
    rank = jnp.sum(from_block * earlier, axis=0, keepdims=True)
    slot_of = origin.astype(jnp.float32) * per_pair + rank
    slot_col = jnp.broadcast_to(slot_of, (rows, rows)).T
    recv_perm[...] = jnp.where(slot_col == col_id.astype(jnp.float32), 1.0, 0.0).astype(jnp.bfloat16)

    for g in range(1, shared):
        relay(g)

    layers = n // reach
    layer = s // reach
    layer_rows = reach * per_pair
    to_place = pl.ds(pl.multiple_of(place * per_pair, per_pair), per_pair)

    def deal_copy(c, e):
        target = lax.rem(s + e * reach, n)
        cut = pl.ds(pl.multiple_of(target // reach * layer_rows, layer_rows), layer_rows)
        return pltpu.make_async_remote_copy(
            src_ref=sendb.at[c, cut], dst_ref=passed.at[c, layer],
            send_sem=deal_send.at[c, e], recv_sem=deal_recv.at[c, e],
            device_id={"seq": target}, device_id_type=MESH,
        )

    def pass_copy(c, e):
        target = lax.rem(place + e, reach)
        cut = pl.ds(pl.multiple_of(target * per_pair, per_pair), per_pair)
        return pltpu.make_async_remote_copy(
            src_ref=passed.at[c, :, cut], dst_ref=arr.at[c, :, to_place],
            send_sem=pass_send.at[c, e], recv_sem=pass_recv.at[c, e],
            device_id={"seq": base + target}, device_id_type=MESH,
        )

    def deal(c):
        loop(1, layers, lambda e: deal_copy(c, e).start())
        keep = pl.ds(pl.multiple_of(layer * layer_rows, layer_rows), layer_rows)
        passed[c, layer] = sendb[c, keep, :]

    def pass_on(c):
        loop(1, layers, lambda e: deal_copy(c, e).wait_recv())
        loop(1, reach, lambda e: pass_copy(c, e).start())
        arr[c, :, to_place, :] = passed[c, :, to_place, :]

    factor = HD ** (-0.5) * 1.4426950408889634

    all_ones = jnp.ones(((reach + 1) * rows, HD), jnp.bfloat16)

    def one_head(g, h, to):
        q = q_sorted[:, pl.ds(pl.multiple_of(h * HD, HD), HD)]
        q = jnp.concatenate([q, query_tag[...]], axis=1)
        scores = [
            dot_nt(q, jnp.concatenate([kv[d, g, :, 0:HD], key_tag[d]], axis=1)) for d in range(reach + 1)
        ]
        is_own = own_first[...] > 0.5
        scores = [jnp.where(is_own, scores[0], scores[reach])] + scores[1:reach]
        peak = jnp.max(functools.reduce(jnp.maximum, scores), axis=1, keepdims=True)
        expo = [jnp.exp2((x - peak) * factor) for x in scores]
        expo = (
            [jnp.where(is_own, expo[0], 0.0)] + expo[1:] + [jnp.where(is_own, 0.0, expo[0])]
        )
        weight = jnp.concatenate([x.astype(jnp.bfloat16) for x in expo], axis=1)
        value = jnp.concatenate([kv[d, g, :, HD : 2 * HD] for d in range(reach + 1)], axis=0)
        update = dot(weight, jnp.concatenate([value, all_ones], axis=1))
        sendb[to, :, pl.ds(pl.multiple_of((h - to * cut_heads) * HD, HD), HD)] = (
            update[:, 0:HD] / update[:, HD : 2 * HD]
        ).astype(jnp.bfloat16)

    for c in range(cuts):
        g = c * cut_heads // per_shared
        if c * cut_heads % per_shared == 0:
            for e in range(1, reach):

                @pl.when(s >= e)
                def _():
                    near_copy(g, e, 0).wait_recv()

        def heads(i):
            w_step = PIECES * TOGETHER // (cuts * cut_heads)
            first = (c * cut_heads // TOGETHER + i) * w_step
            loop(first, first + w_step, lambda j: w_copy(j).start())
            for k in range(TOGETHER):
                one_head(g, c * cut_heads + i * TOGETHER + k, c)

        loop(0, cut_heads // TOGETHER, heads)
        deal(c)
        if c >= 2:
            pass_on(c - 2)

    def wide_cut(c):
        return pl.ds(pl.multiple_of(c * WIDE, WIDE), WIDE)

    def sum_copy(c):
        return pltpu.make_async_remote_copy(
            src_ref=part.at[c, other_half], dst_ref=other.at[c],
            send_sem=sum_send.at[c], recv_sem=sum_recv.at[c],
            device_id={"tp": 1 - t}, device_id_type=MESH,
        )

    def keep_copy(c):
        return pltpu.make_async_copy(part.at[c, own_half], out_ref.at[:, wide_cut(c)], keep_sem.at[c])

    def finish(c):
        sum_copy(c).wait_recv()
        total = part[c, own_half, :].astype(jnp.float32) + other[c].astype(jnp.float32)
        part[c, own_half, :] = total.astype(jnp.bfloat16)
        keep_copy(c).start()

    for g in range(cuts):
        share = PIECES // cuts
        loop(g * share, (g + 1) * share, lambda i: w_copy(i).wait())
        if 0 < g < cuts - 1:
            pass_on(g + 1)
        loop(1, reach, lambda e: pass_copy(g, e).wait_recv())
        mixed[...] = dot(recv_perm[...], arr[g].reshape(rows, depth)).astype(jnp.bfloat16)

        def one_width(c):
            term = dot(mixed[...], wbuf[g * depth : (g + 1) * depth, wide_cut(c)])
            if g > 0:
                term = term + acc[c]
            if g < cuts - 1:
                acc[c] = term
            else:
                part[c] = term.astype(jnp.bfloat16)
                sum_copy(c).start()

                @pl.when(c >= BEHIND)
                def _():
                    finish(c - BEHIND)

        loop(0, wide_count, one_width)

    loop(wide_count - BEHIND, wide_count, finish)
    loop(0, wide_count, lambda c: keep_copy(c).wait())

    for g in range(shared):
        pair_copy(g).wait_send()

        @pl.when(s + reach < n)
        def _():
            far_copy(g).wait_send()

        for e in range(1, reach):

            @pl.when((place + e < reach) | (s >= reach))
            def _():
                near_copy(g, e, 0).wait_send()

    for c in range(cuts):
        loop(1, layers, lambda e: deal_copy(c, e).wait_send())
        loop(1, reach, lambda e: pass_copy(c, e).wait_send())
    loop(0, wide_count, lambda c: sum_copy(c).wait_send())


def copy_kernel(from_ref, to_ref, held, in_sem, out_sem):
    rows = from_ref.shape[0] // COPIES

    def cut(i):
        return pl.ds(i * rows, rows)

    def take(i):
        return pltpu.make_async_copy(from_ref.at[cut(i)], held.at[cut(i)], in_sem.at[i])

    def give(i):
        return pltpu.make_async_copy(held.at[cut(i)], to_ref.at[cut(i)], out_sem.at[i])

    for i in range(COPIES):
        take(i).start()
    for i in range(COPIES):
        take(i).wait()
        give(i).start()
    for i in range(COPIES):
        give(i).wait()


def fused_shards(segment_ids, relayout, queries, keys, values, out_weight):
    n = lax.axis_size("seq")
    rows = queries.shape[0]
    reach = n // LONGEST_SHARE
    shared = keys.shape[1] // HD // 2
    depth = queries.shape[1] // CUTS
    width = out_weight.shape[1]
    wide_count = width // WIDE
    bf16, f32 = jnp.bfloat16, jnp.float32
    dma = pltpu.SemaphoreType.DMA
    vmem = pl.BlockSpec(memory_space=pltpu.VMEM)
    result = pl.pallas_call(
        functools.partial(fused_kernel, n, reach),
        out_shape=jax.ShapeDtypeStruct((rows // 2, width), bf16),
        in_specs=[vmem] * 5 + [pl.BlockSpec(memory_space=pl.ANY)],
        out_specs=pl.BlockSpec(memory_space=pl.ANY),
        scratch_shapes=[
            pltpu.VMEM((n, rows), jnp.int32),
            pltpu.VMEM((n, rows), jnp.int32),
            pltpu.VMEM((reach + 1, shared, rows, 2 * HD), bf16),
            pltpu.VMEM((shared, rows // 2, 2 * HD), bf16),
            pltpu.VMEM((reach + 1, rows, HD), bf16),
            pltpu.VMEM((rows, HD), bf16),
            pltpu.VMEM((rows, rows), f32),
            pltpu.VMEM((rows, rows), bf16),
            pltpu.VMEM((rows, rows), bf16),
            pltpu.VMEM((n, rows), f32),
            pltpu.VMEM(queries.shape, bf16),
            pltpu.VMEM((rows, depth), bf16),
            pltpu.VMEM((CUTS, rows, depth), bf16),
            pltpu.VMEM((CUTS, n // reach, rows * reach // n, depth), bf16),
            pltpu.VMEM((CUTS, n // reach, rows * reach // n, depth), bf16),
            pltpu.VMEM((wide_count, rows, WIDE), f32),
            pltpu.VMEM((wide_count, rows, WIDE), bf16),
            pltpu.VMEM((wide_count, rows // 2, WIDE), bf16),
            pltpu.VMEM(out_weight.shape, bf16),
            dma((PIECES,)),
            dma((shared,)),
            dma((shared,)),
            dma((shared,)),
            dma((shared,)),
            dma((shared, reach)),
            dma((shared, reach)),
            dma((CUTS, n // reach)),
            dma((CUTS, n // reach)),
            dma((CUTS, reach)),
            dma((CUTS, reach)),
            dma((wide_count,)),
            dma((wide_count,)),
            dma((wide_count,)),
        ],
        compiler_params=pltpu.CompilerParams(
            collective_id=0, has_side_effects=True, vmem_limit_bytes=63 * 1024 * 1024
        ),
    )(segment_ids.reshape(-1, 128), relayout.reshape(-1, 128), queries, keys, values, out_weight)
    return pl.pallas_call(
        copy_kernel,
        out_shape=jax.ShapeDtypeStruct(result.shape, bf16),
        in_specs=[pl.BlockSpec(memory_space=pl.ANY)],
        out_specs=pl.BlockSpec(memory_space=pl.ANY),
        scratch_shapes=[pltpu.VMEM(result.shape, bf16), dma((COPIES,)), dma((COPIES,))],
    )(result)


def shards(segment_ids, relayout, queries, keys, values, out_weight):
    rows_here = queries.shape[0]
    seq_count = lax.axis_size("seq")
    seq_index = lax.axis_index("seq")
    tp_index = lax.axis_index("tp")
    total_rows = rows_here * seq_count
    heads_here = queries.shape[1] // HD
    group = QH // KVH
    shared_here = max(1, heads_here // group)
    per_shared = heads_here // shared_here
    scale = HD ** (-0.5)
    all_keys, all_values = (
        lax.all_gather(keys, "tp", axis=0, tiled=True),
        lax.all_gather(values, "tp", axis=0, tiled=True),
    )
    first_head = tp_index * heads_here // group
    own_keys = lax.dynamic_slice_in_dim(all_keys, first_head * HD, shared_here * HD, 1)
    own_values = lax.dynamic_slice_in_dim(all_values, first_head * HD, shared_here * HD, 1)
    own_pair = jnp.stack([own_keys, own_values])
    row_ids = jnp.arange(rows_here, dtype=jnp.int32)
    inverse = (
        jnp.zeros((total_rows,), jnp.int32)
        .at[relayout]
        .set(jnp.arange(total_rows, dtype=jnp.int32))
    )
    new_here = seq_index * rows_here + row_ids
    old_here = seq_index * rows_here + row_ids
    source_block = relayout[new_here] // rows_here
    arrival = jnp.argsort(source_block * total_rows + new_here)
    send_order = jnp.argsort(inverse[old_here])
    arrived = lax.all_to_all(queries[send_order], "seq", split_axis=0, concat_axis=0, tiled=True)
    query_pos = relayout[seq_index * rows_here + arrival]
    query_seg = segment_ids[query_pos]
    pieces = lax.all_gather(own_pair, "seq", axis=1, tiled=True)
    count = pieces.shape[1]
    key_pos = jnp.arange(count, dtype=jnp.int32)
    live = (
        (key_pos[None, :] <= query_pos[:, None])
        & (segment_ids[None, :] == query_seg[:, None])
        & (jnp.int32(0) >= 0)
    )
    query_split = arrived.reshape(rows_here, shared_here, per_shared, HD)
    key_split = pieces[0].reshape(count, shared_here, HD)
    value_split = pieces[1].reshape(count, shared_here, HD)
    scores = (
        jnp.einsum("qngd,knd->ngqk", query_split, key_split, preferred_element_type=jnp.float32)
        * scale
    )
    masked = jnp.where(live, scores, jnp.float32(-1e30))
    peak = jnp.full((shared_here, per_shared, rows_here), -1e30, jnp.float32)
    new_peak = jnp.maximum(peak, jnp.max(masked, axis=-1))
    expo = jnp.where(live, jnp.exp(masked - new_peak[..., None]), jnp.float32(0.0))
    denom = jnp.sum(expo, axis=-1)
    update = jnp.einsum(
        "ngqk,knd->ngqd", expo.astype(jnp.bfloat16), value_split, preferred_element_type=jnp.float32
    )
    attn = update / denom[..., None]
    attn_rows = (
        jnp.transpose(attn, (2, 0, 1, 3)).reshape(rows_here, heads_here * HD).astype(jnp.bfloat16)
    )
    attn_new = jnp.zeros_like(attn_rows).at[arrival].set(attn_rows)
    return lax.psum_scatter(
        jnp.dot(attn_new, out_weight, preferred_element_type=jnp.float32).astype(jnp.bfloat16),
        "tp",
        scatter_dimension=0,
        tiled=True,
    )


def solution(mesh):
    return jax.shard_map(
        fused_shards if mesh.shape["tp"] == 2 else shards,
        mesh=mesh,
        in_specs=(
            P(),
            P(),
            P("seq", "tp"),
            P(("seq", "tp"), None),
            P(("seq", "tp"), None),
            P("tp", None),
        ),
        out_specs=P(("seq", "tp"), None),
        check_vma=False,
    )
```

```python
import functools

import jax
import jax.numpy as jnp
from jax import lax
from jax.experimental import pallas as pl
from jax.experimental.pallas import tpu as pltpu
from jax.sharding import PartitionSpec as P

QH = 32
KVH = 4
HD = 128
LONGEST_SHARE = 4
MESH = pl.DeviceIdType.MESH
WIDE = 1024
PIECES = 8
CUTS = 4
TOGETHER = 2
BEHIND = 4
COPIES = 8


def dot(a, b):
    return jnp.dot(a, b, preferred_element_type=jnp.float32)


def dot_nt(a, b):
    return lax.dot_general(a, b, (((1,), (1,)), ((), ())), preferred_element_type=jnp.float32)


def loop(low, high, body, unroll=1):
    def step(i, carry):
        body(i)
        return carry

    lax.fori_loop(low, high, step, 0, unroll=unroll)


def fused_kernel(
    n, reach, seg_in, lay_in, q_ref, k_ref, v_ref, w_hbm, out_ref,
    seg_ref, lay_ref, kv, stage, key_tag, query_tag, own_first, send_perm, recv_perm, rank_ref, q_sorted,
    mixed, sendb, arr, acc, part, other, wbuf,
    w_sem, pair_send, pair_recv, far_send, far_recv, near_send, near_recv,
    a2a_send, a2a_recv, sum_send, sum_recv, keep_sem,
):
    s = lax.axis_index("seq")
    t = lax.axis_index("tp")
    rows = q_ref.shape[0]
    half = rows // 2
    per_pair = rows // n
    shared = kv.shape[1]
    per_shared = q_ref.shape[1] // HD // shared
    cuts, _, depth = sendb.shape
    cut_heads = depth // HD
    wide_count = acc.shape[0]
    w_rows = w_hbm.shape[0] // PIECES
    place = lax.rem(s, reach)
    base = s - place

    barrier = pltpu.get_barrier_semaphore()
    loop(
        1, n,
        lambda e: pl.semaphore_signal(
            barrier, inc=1, device_id={"seq": lax.rem(s + e, n)}, device_id_type=MESH
        ),
    )
    pl.semaphore_signal(barrier, inc=1, device_id={"tp": 1 - t}, device_id_type=MESH)

    def w_copy(i):
        cut = pl.ds(pl.multiple_of(i * w_rows, w_rows), w_rows)
        return pltpu.make_async_copy(w_hbm.at[cut], wbuf.at[cut], w_sem.at[i])

    own_half = pl.ds(pl.multiple_of(t * half, half), half)
    other_half = pl.ds(pl.multiple_of((1 - t) * half, half), half)
    for g in range(shared):
        mine = pl.ds(pl.multiple_of((t * shared + g) * HD, HD), HD)
        theirs = pl.ds(pl.multiple_of(((1 - t) * shared + g) * HD, HD), HD)
        kv[0, g, own_half, 0:HD] = k_ref[:, mine]
        kv[0, g, own_half, HD : 2 * HD] = v_ref[:, mine]
        stage[g, :, 0:HD] = k_ref[:, theirs]
        stage[g, :, HD : 2 * HD] = v_ref[:, theirs]

    pl.semaphore_wait(barrier, n)

    def pair_copy(g):
        return pltpu.make_async_remote_copy(
            src_ref=stage.at[g], dst_ref=kv.at[0, g, own_half],
            send_sem=pair_send.at[g], recv_sem=pair_recv.at[g],
            device_id={"tp": 1 - t}, device_id_type=MESH,
        )

    def far_copy(g):
        return pltpu.make_async_remote_copy(
            src_ref=kv.at[0, g], dst_ref=kv.at[reach, g],
            send_sem=far_send.at[g], recv_sem=far_recv.at[g],
            device_id={"seq": lax.rem(s + reach, n)}, device_id_type=MESH,
        )

    def near_copy(g, e, slot):
        return pltpu.make_async_remote_copy(
            src_ref=kv.at[slot, g], dst_ref=kv.at[e, g],
            send_sem=near_send.at[g, e], recv_sem=near_recv.at[g, e],
            device_id={"seq": base + lax.rem(place + e, reach)}, device_id_type=MESH,
        )

    def own_out(g):
        pair_copy(g).wait_recv()

        @pl.when(s + reach < n)
        def _():
            far_copy(g).start()

        for e in range(1, reach):

            @pl.when(place + e < reach)
            def _():
                near_copy(g, e, 0).start()

    def relay(g):
        @pl.when(s >= reach)
        def _():
            far_copy(g).wait_recv()
            for e in range(1, reach):

                @pl.when(place + e >= reach)
                def _():
                    near_copy(g, e, reach).start()

    for g in range(shared):
        pair_copy(g).start()
    for e in range(1, reach + 1):

        @pl.when(s < e)
        def _():
            kv[e] = jnp.zeros_like(kv[e])

    own_out(0)
    loop(0, PIECES, lambda i: w_copy(i).start())

    lines = rows // 128
    for ref, source in ((seg_ref, seg_in), (lay_ref, lay_in)):
        for i in range(lines):
            ref[:, i * 128 : (i + 1) * 128] = source[pl.ds(i, n, stride=lines), :]

    tag_id = lax.broadcasted_iota(jnp.int32, (rows, HD), 1)
    for d in range(reach + 1):
        key_seg = jnp.where(s >= d, seg_ref[pl.ds(jnp.maximum(s - d, 0), 1), :], HD - 1)
        key_col = jnp.broadcast_to(key_seg, (HD, rows)).T
        key_tag[d] = jnp.where(key_col == tag_id, 1.0, 0.0).astype(jnp.bfloat16)

    relay(0)
    for g in range(1, shared):
        own_out(g)

    row_id = lax.broadcasted_iota(jnp.int32, (rows, rows), 0)
    col_id = lax.broadcasted_iota(jnp.int32, (rows, rows), 1)

    before = jnp.where(row_id < col_id, 1.0, 0.0).astype(jnp.bfloat16)
    local = lay_ref[...] - s * rows
    is_mine = (local >= 0) & (local < rows)
    ranks = dot(jnp.where(is_mine, 1.0, 0.0).astype(jnp.bfloat16), before)
    rank_ref[...] = jnp.where(is_mine, ranks, -1.0)
    rank_id = lax.broadcasted_iota(jnp.int32, (per_pair, rows), 0).astype(jnp.float32)

    def one_target(b):
        pick = jnp.where(rank_ref[pl.ds(b, 1), :] == rank_id, 1.0, 0.0).astype(jnp.bfloat16)
        token = jnp.where(lay_ref[pl.ds(b, 1), :] - s * rows == row_id, 1.0, 0.0).astype(jnp.bfloat16)
        cut = pl.ds(pl.multiple_of(b * per_pair, per_pair), per_pair)
        send_perm[cut, :] = dot_nt(pick, token).astype(jnp.bfloat16)

    loop(0, n, one_target, unroll=4)

    def sort_queries(c):
        cut = pl.ds(pl.multiple_of(c * depth, depth), depth)
        q_sorted[:, cut] = dot(send_perm[...], q_ref[:, cut]).astype(jnp.bfloat16)

    loop(0, cuts, sort_queries)
    chosen = send_perm[...].astype(jnp.float32)
    position = jnp.sum(chosen * col_id.astype(jnp.float32), axis=1, keepdims=True)
    document = jnp.sum(chosen * seg_ref[pl.ds(s, 1), :].astype(jnp.float32), axis=1, keepdims=True)
    query_tag[...] = jnp.where(document == tag_id.astype(jnp.float32), 0.0, -1e30).astype(jnp.bfloat16)
    own_first[...] = jnp.where(col_id.astype(jnp.float32) <= position, 1.0, 0.0)


    for g in range(1, shared):
        relay(g)

    def a2a_copy(g, e):
        target = lax.rem(s + e, n)
        return pltpu.make_async_remote_copy(
            src_ref=sendb.at[g, pl.ds(pl.multiple_of(target * per_pair, per_pair), per_pair)],
            dst_ref=arr.at[g, pl.ds(pl.multiple_of(s * per_pair, per_pair), per_pair)],
            send_sem=a2a_send.at[g, e], recv_sem=a2a_recv.at[g, e],
            device_id={"seq": target}, device_id_type=MESH,
        )

    factor = HD ** (-0.5) * 1.4426950408889634

    all_ones = jnp.ones(((reach + 1) * rows, HD), jnp.bfloat16)

    def one_head(g, h, to):
        q = q_sorted[:, pl.ds(pl.multiple_of(h * HD, HD), HD)]
        q = jnp.concatenate([q, query_tag[...]], axis=1)
        scores = [
            dot_nt(q, jnp.concatenate([kv[d, g, :, 0:HD], key_tag[d]], axis=1)) for d in range(reach + 1)
        ]
        is_own = own_first[...] > 0.5
        scores = [jnp.where(is_own, scores[0], scores[reach])] + scores[1:reach]
        peak = jnp.max(functools.reduce(jnp.maximum, scores), axis=1, keepdims=True)
        expo = [jnp.exp2((x - peak) * factor) for x in scores]
        expo = (
            [jnp.where(is_own, expo[0], 0.0)] + expo[1:] + [jnp.where(is_own, 0.0, expo[0])]
        )
        weight = jnp.concatenate([x.astype(jnp.bfloat16) for x in expo], axis=1)
        value = jnp.concatenate([kv[d, g, :, HD : 2 * HD] for d in range(reach + 1)], axis=0)
        update = dot(weight, jnp.concatenate([value, all_ones], axis=1))
        sendb[to, :, pl.ds(pl.multiple_of((h - to * cut_heads) * HD, HD), HD)] = (
            update[:, 0:HD] / update[:, HD : 2 * HD]
        ).astype(jnp.bfloat16)

    for c in range(cuts):
        g = c * cut_heads // per_shared
        if c * cut_heads % per_shared == 0:
            for e in range(1, reach):

                @pl.when(s >= e)
                def _():
                    near_copy(g, e, 0).wait_recv()

        def heads(i):
            for k in range(TOGETHER):
                one_head(g, c * cut_heads + i * TOGETHER + k, c)

        loop(0, cut_heads // TOGETHER, heads)
        loop(1, n, lambda e: a2a_copy(c, e).start())
        keep = pl.ds(pl.multiple_of(s * per_pair, per_pair), per_pair)
        arr[c, keep, :] = sendb[c, keep, :]

    origin = lay_ref[pl.ds(s, 1), :] // rows
    block_id = lax.broadcasted_iota(jnp.int32, (n, rows), 0)
    from_block = jnp.where(origin == block_id, 1.0, 0.0)
    earlier = dot(from_block.astype(jnp.bfloat16), before)
    rank = jnp.sum(from_block * earlier, axis=0, keepdims=True)
    slot_of = origin.astype(jnp.float32) * per_pair + rank
    slot_col = jnp.broadcast_to(slot_of, (rows, rows)).T
    recv_perm[...] = jnp.where(slot_col == col_id.astype(jnp.float32), 1.0, 0.0).astype(jnp.bfloat16)

    def wide_cut(c):
        return pl.ds(pl.multiple_of(c * WIDE, WIDE), WIDE)

    def sum_copy(c):
        return pltpu.make_async_remote_copy(
            src_ref=part.at[c, other_half], dst_ref=other.at[c],
            send_sem=sum_send.at[c], recv_sem=sum_recv.at[c],
            device_id={"tp": 1 - t}, device_id_type=MESH,
        )

    def keep_copy(c):
        return pltpu.make_async_copy(part.at[c, own_half], out_ref.at[:, wide_cut(c)], keep_sem.at[c])

    def finish(c):
        sum_copy(c).wait_recv()
        total = part[c, own_half, :].astype(jnp.float32) + other[c].astype(jnp.float32)
        part[c, own_half, :] = total.astype(jnp.bfloat16)
        keep_copy(c).start()

    for g in range(cuts):
        share = PIECES // cuts
        loop(g * share, (g + 1) * share, lambda i: w_copy(i).wait())
        loop(1, n, lambda e: a2a_copy(g, e).wait_recv())
        mixed[...] = dot(recv_perm[...], arr[g]).astype(jnp.bfloat16)

        def one_width(c):
            term = dot(mixed[...], wbuf[g * depth : (g + 1) * depth, wide_cut(c)])
            if g > 0:
                term = term + acc[c]
            if g < cuts - 1:
                acc[c] = term
            else:
                part[c] = term.astype(jnp.bfloat16)
                sum_copy(c).start()

                @pl.when(c >= BEHIND)
                def _():
                    finish(c - BEHIND)

        loop(0, wide_count, one_width)

    loop(wide_count - BEHIND, wide_count, finish)
    loop(0, wide_count, lambda c: keep_copy(c).wait())

    for g in range(shared):
        pair_copy(g).wait_send()

        @pl.when(s + reach < n)
        def _():
            far_copy(g).wait_send()

        for e in range(1, reach):

            @pl.when((place + e < reach) | (s >= reach))
            def _():
                near_copy(g, e, 0).wait_send()

    for c in range(cuts):
        loop(1, n, lambda e: a2a_copy(c, e).wait_send())
    loop(0, wide_count, lambda c: sum_copy(c).wait_send())


def copy_kernel(from_ref, to_ref, held, in_sem, out_sem):
    rows = from_ref.shape[0] // COPIES

    def cut(i):
        return pl.ds(i * rows, rows)

    def take(i):
        return pltpu.make_async_copy(from_ref.at[cut(i)], held.at[cut(i)], in_sem.at[i])

    def give(i):
        return pltpu.make_async_copy(held.at[cut(i)], to_ref.at[cut(i)], out_sem.at[i])

    for i in range(COPIES):
        take(i).start()
    for i in range(COPIES):
        take(i).wait()
        give(i).start()
    for i in range(COPIES):
        give(i).wait()


def fused_shards(segment_ids, relayout, queries, keys, values, out_weight):
    n = lax.axis_size("seq")
    rows = queries.shape[0]
    reach = n // LONGEST_SHARE
    shared = keys.shape[1] // HD // 2
    depth = queries.shape[1] // CUTS
    width = out_weight.shape[1]
    wide_count = width // WIDE
    bf16, f32 = jnp.bfloat16, jnp.float32
    dma = pltpu.SemaphoreType.DMA
    vmem = pl.BlockSpec(memory_space=pltpu.VMEM)
    result = pl.pallas_call(
        functools.partial(fused_kernel, n, reach),
        out_shape=jax.ShapeDtypeStruct((rows // 2, width), bf16),
        in_specs=[vmem] * 5 + [pl.BlockSpec(memory_space=pl.ANY)],
        out_specs=pl.BlockSpec(memory_space=pl.ANY),
        scratch_shapes=[
            pltpu.VMEM((n, rows), jnp.int32),
            pltpu.VMEM((n, rows), jnp.int32),
            pltpu.VMEM((reach + 1, shared, rows, 2 * HD), bf16),
            pltpu.VMEM((shared, rows // 2, 2 * HD), bf16),
            pltpu.VMEM((reach + 1, rows, HD), bf16),
            pltpu.VMEM((rows, HD), bf16),
            pltpu.VMEM((rows, rows), f32),
            pltpu.VMEM((rows, rows), bf16),
            pltpu.VMEM((rows, rows), bf16),
            pltpu.VMEM((n, rows), f32),
            pltpu.VMEM(queries.shape, bf16),
            pltpu.VMEM((rows, depth), bf16),
            pltpu.VMEM((CUTS, rows, depth), bf16),
            pltpu.VMEM((CUTS, rows, depth), bf16),
            pltpu.VMEM((wide_count, rows, WIDE), f32),
            pltpu.VMEM((wide_count, rows, WIDE), bf16),
            pltpu.VMEM((wide_count, rows // 2, WIDE), bf16),
            pltpu.VMEM(out_weight.shape, bf16),
            dma((PIECES,)),
            dma((shared,)),
            dma((shared,)),
            dma((shared,)),
            dma((shared,)),
            dma((shared, reach)),
            dma((shared, reach)),
            dma((CUTS, n)),
            dma((CUTS, n)),
            dma((wide_count,)),
            dma((wide_count,)),
            dma((wide_count,)),
        ],
        compiler_params=pltpu.CompilerParams(
            collective_id=0, has_side_effects=True, vmem_limit_bytes=63 * 1024 * 1024
        ),
    )(segment_ids.reshape(-1, 128), relayout.reshape(-1, 128), queries, keys, values, out_weight)
    return pl.pallas_call(
        copy_kernel,
        out_shape=jax.ShapeDtypeStruct(result.shape, bf16),
        in_specs=[pl.BlockSpec(memory_space=pl.ANY)],
        out_specs=pl.BlockSpec(memory_space=pl.ANY),
        scratch_shapes=[pltpu.VMEM(result.shape, bf16), dma((COPIES,)), dma((COPIES,))],
    )(result)


def shards(segment_ids, relayout, queries, keys, values, out_weight):
    rows_here = queries.shape[0]
    seq_count = lax.axis_size("seq")
    seq_index = lax.axis_index("seq")
    tp_index = lax.axis_index("tp")
    total_rows = rows_here * seq_count
    heads_here = queries.shape[1] // HD
    group = QH // KVH
    shared_here = max(1, heads_here // group)
    per_shared = heads_here // shared_here
    scale = HD ** (-0.5)
    all_keys, all_values = (
        lax.all_gather(keys, "tp", axis=0, tiled=True),
        lax.all_gather(values, "tp", axis=0, tiled=True),
    )
    first_head = tp_index * heads_here // group
    own_keys = lax.dynamic_slice_in_dim(all_keys, first_head * HD, shared_here * HD, 1)
    own_values = lax.dynamic_slice_in_dim(all_values, first_head * HD, shared_here * HD, 1)
    own_pair = jnp.stack([own_keys, own_values])
    row_ids = jnp.arange(rows_here, dtype=jnp.int32)
    inverse = (
        jnp.zeros((total_rows,), jnp.int32)
        .at[relayout]
        .set(jnp.arange(total_rows, dtype=jnp.int32))
    )
    new_here = seq_index * rows_here + row_ids
    old_here = seq_index * rows_here + row_ids
    source_block = relayout[new_here] // rows_here
    arrival = jnp.argsort(source_block * total_rows + new_here)
    send_order = jnp.argsort(inverse[old_here])
    arrived = lax.all_to_all(queries[send_order], "seq", split_axis=0, concat_axis=0, tiled=True)
    query_pos = relayout[seq_index * rows_here + arrival]
    query_seg = segment_ids[query_pos]
    pieces = lax.all_gather(own_pair, "seq", axis=1, tiled=True)
    count = pieces.shape[1]
    key_pos = jnp.arange(count, dtype=jnp.int32)
    live = (
        (key_pos[None, :] <= query_pos[:, None])
        & (segment_ids[None, :] == query_seg[:, None])
        & (jnp.int32(0) >= 0)
    )
    query_split = arrived.reshape(rows_here, shared_here, per_shared, HD)
    key_split = pieces[0].reshape(count, shared_here, HD)
    value_split = pieces[1].reshape(count, shared_here, HD)
    scores = (
        jnp.einsum("qngd,knd->ngqk", query_split, key_split, preferred_element_type=jnp.float32)
        * scale
    )
    masked = jnp.where(live, scores, jnp.float32(-1e30))
    peak = jnp.full((shared_here, per_shared, rows_here), -1e30, jnp.float32)
    new_peak = jnp.maximum(peak, jnp.max(masked, axis=-1))
    expo = jnp.where(live, jnp.exp(masked - new_peak[..., None]), jnp.float32(0.0))
    denom = jnp.sum(expo, axis=-1)
    update = jnp.einsum(
        "ngqk,knd->ngqd", expo.astype(jnp.bfloat16), value_split, preferred_element_type=jnp.float32
    )
    attn = update / denom[..., None]
    attn_rows = (
        jnp.transpose(attn, (2, 0, 1, 3)).reshape(rows_here, heads_here * HD).astype(jnp.bfloat16)
    )
    attn_new = jnp.zeros_like(attn_rows).at[arrival].set(attn_rows)
    return lax.psum_scatter(
        jnp.dot(attn_new, out_weight, preferred_element_type=jnp.float32).astype(jnp.bfloat16),
        "tp",
        scatter_dimension=0,
        tiled=True,
    )


def solution(mesh):
    return jax.shard_map(
        fused_shards if mesh.shape["tp"] == 2 else shards,
        mesh=mesh,
        in_specs=(
            P(),
            P(),
            P("seq", "tp"),
            P(("seq", "tp"), None),
            P(("seq", "tp"), None),
            P("tp", None),
        ),
        out_specs=P(("seq", "tp"), None),
        check_vma=False,
    )
```
